256 devices in a mesh: seq: 64 (over y_hi, x, z), head: 4 (over y_lo, core).
Axes of the slice: x: 4, y: 4 (y_hi: 2, y_lo: 2; y = y_hi * 2 + y_lo), z: 8, core: 2. Of those that a mesh axis runs over, the one named last changes fastest.
Arguments:
- tokens: bfloat16 [131072, 768], P(('seq', 'head')), may hold values from -6 to 6
- cotangent: bfloat16 [131072, 768], P(('seq', 'head')), may hold values from -6 to 6
- w_query: bfloat16 [768, 768], P('head'), may hold values from -0.21875 to 0.21875
- w_key: bfloat16 [768, 768], P('head'), may hold values from -0.21875 to 0.21875
- w_value: bfloat16 [768, 768], P('head'), may hold values from -0.21875 to 0.21875
- w_out: bfloat16 [768, 768], P('head'), may hold values from -0.21875 to 0.21875
- offsets: int32 [3, 12], replicated, may hold values from 0 to 127, as said below
Outputs:
- mixed: bfloat16 [131072, 768], P(('seq', 'head'))
- grad_tokens: bfloat16 [131072, 768], P(('seq', 'head'))
- grad_query: float32 [768, 768], P('head')
- grad_key: float32 [768, 768], P('head')
- grad_value: float32 [768, 768], P('head')
- grad_out: float32 [768, 768], P('head')
The draws below stay inside these ranges and needn't reach their ends.
Inputs may be any that keep to these rules, and one draw needn't show every extreme that they name: Row l of offsets lies in 0 to the dilation of level l + 1 minus 1; in every row some head has 0 and some head has the row's largest allowed value.
All inputs are finite; a program needn't handle non-finite values.
Results may differ from the reference program's by a relative error of at most 0.017.
Values may be sent and summed in bfloat16 or wider, within the bound.
No kernel may reach another device: no remote copies, remote signals or barrier semaphores. Data moves between devices by JAX's collectives and lax.ppermute only.
A program may use at most 128 MiB of HBM per device.

```python
import jax
import jax.numpy as jnp
from jax import lax

D = 768
HEADS = 12
HEAD_DIM = 64
TOKENS_PER_INDEX = 2048
SEL = 512
SPAN_SECOND = 8
SPAN_THIRD = 32
DILATION_FIRST = 8
DILATION_SECOND = 32
DILATION_THIRD = 128
TOKENS = 131072
N_HEAD = 4


def draw_offsets(key, part):
    key = jax.random.fold_in(key, 7)
    base_key, spot_key = jax.random.split(key)
    segment_bounds = jnp.array([DILATION_FIRST, DILATION_SECOND, DILATION_THIRD], dtype=jnp.int32)[:, None]
    base = jax.random.randint(base_key, (3, HEADS), 0, segment_bounds, dtype=jnp.int32)
    head_ids = jnp.arange(HEADS, dtype=jnp.int32)[None, :]
    spots = jnp.stack([jax.random.permutation(level_key, HEADS)[:2] for level_key in jax.random.split(spot_key, 3)]).astype(jnp.int32)
    at_top = head_ids == spots[:, 0:1]
    at_bottom = head_ids == spots[:, 1:2]
    return jnp.where(at_top, segment_bounds - 1, jnp.where(at_bottom, 0, base)).astype(jnp.int32)


def steps_of(stream_key, dims, cuts, smallest, high):
    gain, own = 1.0, jax.random.fold_in(stream_key, 6)
    for position, shards_of in cuts:
        draws = jnp.exp(jax.random.uniform(jax.random.fold_in(own, position), (shards_of,), jnp.float32, smallest / len(cuts), high / len(cuts)))
        gain = gain * jnp.repeat(draws, dims[position] // shards_of).reshape([-1 if axis == position else 1 for axis in range(len(dims))])
    return gain


def gaussian(stream_key, shape, deviation, most, cuts=(), held_as=jnp.bfloat16):
    result = jax.random.normal(stream_key, shape, jnp.float32) * deviation
    if len(cuts) > 0:
        result = steps_of(stream_key, shape, cuts, -0.22, 0.18) * result
    return jnp.clip(result, min=-most, max=most).astype(held_as)


def setup_inputs(seed: int = 0) -> dict:
    seeds = jax.random.split(jax.random.key(seed), 8)
    return {
        "tokens": gaussian(seeds[0], (TOKENS, D), 1.0, 6.0, ((0, 256),)),
        "cotangent": gaussian(seeds[1], (TOKENS, D), 1.0, 6.0, ((0, 256),)),
        "w_query": gaussian(seeds[2], (D, D), D ** -0.5, 0.21875, ((0, 4),)),
        "w_key": gaussian(seeds[3], (D, D), D ** -0.5, 0.21875, ((0, 4),)),
        "w_value": gaussian(seeds[4], (D, D), D ** -0.5, 0.21875, ((0, 4),)),
        "w_out": gaussian(seeds[5], (D, D), D ** -0.5, 0.21875, ((0, 4),)),
        "offsets": draw_offsets(jax.random.fold_in(seeds[7], 71), 0),
    }


def pick_rows(field, dilation, offset):
    shaped = field.reshape(-1, dilation, field.shape[-1])
    return lax.dynamic_slice_in_dim(shaped, offset.astype(jnp.int32), 1, 1)[:, 0]


def spread_back(packed, dilation, offset):
    selected = jnp.arange(dilation, dtype=jnp.int32) == offset.astype(jnp.int32)
    full_rows = jnp.where(selected[None, :, None], packed[:, None, :], jnp.zeros((), packed.dtype))
    return full_rows.reshape(-1, packed.shape[-1])


def head_pass(query_head, key_head, value_head, grad_head, head_offsets):
    dilation_levels = ((2 * TOKENS_PER_INDEX, DILATION_FIRST), (SPAN_SECOND * TOKENS_PER_INDEX, DILATION_SECOND), (SPAN_THIRD * TOKENS_PER_INDEX, DILATION_THIRD))
    score_scale = HEAD_DIM ** -0.5
    totals = jnp.zeros((TOKENS,), jnp.float32)
    covered = jnp.zeros((TOKENS,), bool)
    stored = []
    for level_id in range(3):
        segment, dilation = dilation_levels[level_id]
        segments = TOKENS // segment
        offset = head_offsets[level_id]
        query_sel = pick_rows(query_head, dilation, offset).reshape(segments, SEL, HEAD_DIM).astype(jnp.float32)
        key_sel = pick_rows(key_head, dilation, offset).reshape(segments, SEL, HEAD_DIM).astype(jnp.float32)
        value_sel = pick_rows(value_head, dilation, offset).reshape(segments, SEL, HEAD_DIM).astype(jnp.float32)
        scores = jnp.einsum("nqe,nke->nqk", query_sel, key_sel) * score_scale
        exponent = jnp.exp(scores)
        totals = totals + spread_back(jnp.sum(exponent, -1).reshape(-1, 1), dilation, offset)[:, 0]
        covered = covered | ((jnp.arange(TOKENS, dtype=jnp.int32) % dilation) == offset.astype(jnp.int32))
        stored.append((segments, dilation, offset, query_sel, key_sel, value_sel, exponent))
    totals = totals + jnp.where(covered, 0.0, 1.0).astype(jnp.float32)
    attended = jnp.zeros((TOKENS, HEAD_DIM), jnp.float32)
    weights_list = []
    for level_id in range(3):
        segments, dilation, offset, query_sel, key_sel, value_sel, exponent = stored[level_id]
        row_totals = pick_rows(totals[:, None], dilation, offset).reshape(segments, SEL)
        weights = exponent / row_totals[:, :, None]
        rounded = lax.optimization_barrier(weights.astype(jnp.bfloat16)).astype(jnp.float32)
        level_part = jnp.einsum("nqk,nke->nqe", rounded, value_sel).reshape(-1, HEAD_DIM)
        attended = attended + spread_back(level_part, dilation, offset)
        weights_list.append((weights, rounded))
    row_delta = jnp.sum(grad_head.astype(jnp.float32) * attended, -1)
    query_grad = jnp.zeros((TOKENS, HEAD_DIM), jnp.float32)
    key_grad = jnp.zeros((TOKENS, HEAD_DIM), jnp.float32)
    value_grad = jnp.zeros((TOKENS, HEAD_DIM), jnp.float32)
    for level_id in range(3):
        segments, dilation, offset, query_sel, key_sel, value_sel, exponent = stored[level_id]
        weights, rounded = weights_list[level_id]
        grad_sel = pick_rows(grad_head, dilation, offset).reshape(segments, SEL, HEAD_DIM).astype(jnp.float32)
        delta_sel = pick_rows(row_delta[:, None], dilation, offset).reshape(segments, SEL)
        grad_weights = jnp.einsum("nqe,nke->nqk", grad_sel, value_sel)
        grad_scores = weights * (grad_weights - delta_sel[:, :, None]) * score_scale
        grad_scores = lax.optimization_barrier(grad_scores.astype(jnp.bfloat16)).astype(jnp.float32)
        query_part = jnp.einsum("nqk,nke->nqe", grad_scores, key_sel).reshape(-1, HEAD_DIM)
        key_part = jnp.einsum("nqk,nqe->nke", grad_scores, query_sel).reshape(-1, HEAD_DIM)
        value_part = jnp.einsum("nqk,nqe->nke", rounded, grad_sel).reshape(-1, HEAD_DIM)
        query_grad = query_grad + spread_back(query_part, dilation, offset)
        key_grad = key_grad + spread_back(key_part, dilation, offset)
        value_grad = value_grad + spread_back(value_part, dilation, offset)
    return attended, query_grad, key_grad, value_grad


def reference(tokens, cotangent, w_query, w_key, w_value, w_out, offsets):
    queries = jnp.dot(tokens, w_query.T, preferred_element_type=jnp.float32).astype(jnp.bfloat16)
    keys = jnp.dot(tokens, w_key.T, preferred_element_type=jnp.float32).astype(jnp.bfloat16)
    values = jnp.dot(tokens, w_value.T, preferred_element_type=jnp.float32).astype(jnp.bfloat16)
    grad_attention = jnp.dot(cotangent, w_out.T, preferred_element_type=jnp.float32).astype(jnp.bfloat16)
    attended_cols = []
    query_cols = []
    key_cols = []
    value_cols = []
    for head_id in range(HEADS):
        lower = head_id * HEAD_DIM
        upper = lower + HEAD_DIM
        results = head_pass(queries[:, lower:upper], keys[:, lower:upper], values[:, lower:upper], grad_attention[:, lower:upper], offsets[:, head_id])
        attended_cols.append(results[0])
        query_cols.append(results[1])
        key_cols.append(results[2])
        value_cols.append(results[3])
    attended = jnp.concatenate(attended_cols, 1)
    attention_out = attended.astype(jnp.bfloat16)
    query_change = jnp.concatenate(query_cols, 1).astype(jnp.bfloat16)
    key_change = jnp.concatenate(key_cols, 1).astype(jnp.bfloat16)
    value_change = jnp.concatenate(value_cols, 1).astype(jnp.bfloat16)
    group_width = D // N_HEAD
    mixed = jnp.zeros((TOKENS, D), jnp.float32)
    grad_tokens = jnp.zeros((TOKENS, D), jnp.float32)
    for group_id in range(N_HEAD):
        lower = group_id * group_width
        upper = lower + group_width
        group_term = jnp.dot(attention_out[:, lower:upper], w_out[lower:upper, :], preferred_element_type=jnp.float32)
        mixed = mixed + lax.optimization_barrier(group_term.astype(jnp.bfloat16)).astype(jnp.float32)
        input_term = jnp.dot(query_change[:, lower:upper], w_query[lower:upper, :], preferred_element_type=jnp.float32)
        input_term = input_term + jnp.dot(key_change[:, lower:upper], w_key[lower:upper, :], preferred_element_type=jnp.float32)
        input_term = input_term + jnp.dot(value_change[:, lower:upper], w_value[lower:upper, :], preferred_element_type=jnp.float32)
        grad_tokens = grad_tokens + lax.optimization_barrier(input_term.astype(jnp.bfloat16)).astype(jnp.float32)
    grad_out = jnp.dot(attention_out.T, cotangent, preferred_element_type=jnp.float32)
    grad_query = jnp.dot(query_change.T, tokens, preferred_element_type=jnp.float32)
    grad_key = jnp.dot(key_change.T, tokens, preferred_element_type=jnp.float32)
    grad_value = jnp.dot(value_change.T, tokens, preferred_element_type=jnp.float32)
    return mixed.astype(jnp.bfloat16), grad_tokens.astype(jnp.bfloat16), grad_query, grad_key, grad_value, grad_out
```

```python
import functools

import jax
import jax.numpy as jnp
from jax import lax
from jax.experimental import pallas as pl
from jax.experimental.pallas import tpu as pltpu
from jax.sharding import PartitionSpec as P

BF = jnp.bfloat16
F32 = jnp.float32
WIDTH = 768
ROWS = 512
SLOT = 256
PER_HEAD = 336
SPANS = ((0, 256), (256, 320), (320, 336))
SCALE = 0.125
HEAD_AXES = ("yl", "core")


def nn(a, b):
    return jnp.dot(a, b, preferred_element_type=F32)


def nt(a, b):
    return lax.dot_general(a, b, (((1,), (1,)), ((), ())), preferred_element_type=F32)


def tn(a, b):
    return lax.dot_general(a, b, (((0,), (0,)), ((), ())), preferred_element_type=F32)


def iota(shape, dim):
    return lax.broadcasted_iota(jnp.int32, shape, dim)


def ones_where(mask):
    return jnp.where(mask, 1.0, 0.0).astype(BF)


def pick_first(offs, group):
    row, col = iota((64, ROWS), 0), iota((64, ROWS), 1)
    return jnp.concatenate([ones_where(8 * row + offs[0, 3 * group + a] == col) for a in range(3)], 0)


def pick_rest(offs, group):
    row, col = iota((16, ROWS), 0), iota((16, ROWS), 1)
    parts = [ones_where(32 * row + offs[1, 3 * group + a] == col) for a in range(3)]
    third = [offs[2, 3 * group + a] for a in range(3)]
    off = jnp.where(row < 4, third[0], jnp.where(row < 8, third[1], jnp.where(row < 12, third[2], 4 * ROWS)))
    parts.append(ones_where(128 * (row & 3) + off == col))
    return jnp.concatenate(parts, 0)


def spread_matrix(offs, group):
    lane = iota((1, SLOT), 1)
    o = [[offs[level, 3 * group + a] for a in range(3)] for level in range(3)]
    first = 8 * (lane & 63) + jnp.where(lane < 64, o[0][0], jnp.where(lane < 128, o[0][1], o[0][2]))
    second = 32 * (lane & 15) + jnp.where(lane < 208, o[1][0], jnp.where(lane < 224, o[1][1], o[1][2]))
    third = 128 * (lane & 3) + jnp.where(
        lane < 244, o[2][0], jnp.where(lane < 248, o[2][1], jnp.where(lane < 252, o[2][2], 4 * ROWS))
    )
    pos = jnp.where(lane < 192, first, jnp.where(lane < 240, second, third))
    return ones_where(iota((ROWS, SLOT), 0) == pos)


def third_order(dim):
    new, old = iota((64, 64), dim), iota((64, 64), 1 - dim)
    source = 16 * ((new >> 2) & 3) + 4 * (new >> 4) + (new & 3)
    return ones_where((source == old) & (new < 48))


def call(body, outs, scratch=(), smem=0, flops=0, nbytes=4 << 20):
    def run(*args):
        vmem = pl.BlockSpec(memory_space=pltpu.VMEM)
        specs = [pl.BlockSpec(memory_space=pltpu.SMEM)] * smem + [vmem] * (len(args) - smem)
        return pl.pallas_call(
            body,
            out_shape=tuple(jax.ShapeDtypeStruct(shape, kind) for shape, kind in outs),
            in_specs=specs,
            out_specs=tuple(vmem for _ in outs),
            scratch_shapes=[pltpu.VMEM(shape, kind) for shape, kind in scratch],
            compiler_params=pltpu.CompilerParams(vmem_limit_bytes=40 << 20),
            cost_estimate=pl.CostEstimate(flops=flops, bytes_accessed=nbytes, transcendentals=0),
        )(*args)

    return run


def pick_kernel(first, rest, offs, where, source, *outs):
    for k in (2, 3, 1, 0):
        group = where[0] ^ k
        parts = ([pick_first(offs, group)] if first else []) + ([pick_rest(offs, group)] if rest else [])
        outs[k][...] = nn(jnp.concatenate(parts, 0), source[...]).astype(BF)


def regroup_rest(rests, whole):
    third = jnp.concatenate([rest[48:64] for rest in rests], 0)
    third = nn(third_order(0), third).astype(BF)
    for a in range(3):
        for k in range(4):
            whole[80 * a + 16 * k : 80 * a + 16 * k + 16] = rests[k][16 * a : 16 * a + 16]
        whole[80 * a + 64 : 80 * a + 80] = third[16 * a : 16 * a + 16]


def regroup_first(firsts, whole):
    for a in range(3):
        for k in range(4):
            whole[256 * a + 64 * k : 256 * a + 64 * k + 64] = firsts[k][64 * a : 64 * a + 64]


def ungroup(parts, slots):
    third = jnp.concatenate([part[320:336] for part in parts] + [jnp.zeros((16, WIDTH), BF)], 0)
    third = nn(third_order(1), third).astype(BF)
    for k in range(4):
        for a in range(3):
            slots[k][64 * a : 64 * a + 64] = parts[a][64 * k : 64 * k + 64]
            slots[k][192 + 16 * a : 208 + 16 * a] = parts[a][256 + 16 * k : 272 + 16 * k]
        slots[k][240:256] = third[16 * k : 16 * k + 16]


def join_kernel(w_query, w_key, w_value, joined):
    for a in range(3):
        own = slice(64 * a, 64 * a + 64)
        joined[256 * a : 256 * a + 64] = w_key[own]
        joined[256 * a + 64 : 256 * a + 128] = w_value[own]
        joined[256 * a + 128 : 256 * a + 192] = w_query[own]
        joined[256 * a + 192 : 256 * a + 256] = jnp.zeros((64, WIDTH), BF)


def pad_out(w_out, a):
    return jnp.concatenate([jnp.zeros((64, WIDTH), BF), w_out[64 * a : 64 * a + 64]], 0)


def project_rest_kernel(x0, x1, x2, x3, joined, whole, query, rest):
    regroup_rest((x0, x1, x2, x3), whole)
    for a in range(3):
        made = nt(whole[80 * a : 80 * a + 80], joined[256 * a : 256 * a + 256]).astype(BF)
        query[80 * a : 80 * a + 80] = made[:, 128:256]
        for k in range(8):
            rest[k, 64 * a : 64 * a + 64] = made[0:64, 0:128]
            rest[k, 192 + 16 * a : 208 + 16 * a] = made[64:80, 0:128]


def project_first_kernel(x0, x1, x2, x3, joined, whole, query, first):
    regroup_first((x0, x1, x2, x3), whole)
    for a in range(3):
        own = slice(256 * a, 256 * a + 256)
        made = nt(whole[own], joined[own]).astype(BF)
        query[own] = made[:, 128:256]
        first[own] = made[:, 0:128]


def rows_of(first, rest, a):
    return jnp.concatenate([first[256 * a : 256 * a + 256], rest[80 * a : 80 * a + 80]], 0)


def grad_rows_kernel(c0, c1, c2, c3, w_out, whole_first, whole_rest, grads):
    slots = (c0, c1, c2, c3)
    regroup_first(slots, whole_first)
    regroup_rest([slot.at[192:256] for slot in slots], whole_rest)
    for a in range(3):
        base = PER_HEAD * a
        grads[base : base + PER_HEAD] = nt(rows_of(whole_first, whole_rest, a), pad_out(w_out, a)).astype(BF)


def attention_kernel(offs, where, query_first, query_rest, grads, first_own, first_other, rest, *refs):
    thirds = refs[:3]
    attended, query_grad, first_back, first_send, second_back = refs[3:8]
    third_back, keys = refs[8:12], refs[12]
    for a in range(3):
        keys[a, 0:256] = first_own[256 * a : 256 * a + 256]
        keys[a, 256:512] = first_other[256 * a : 256 * a + 256]
        for k in range(8):
            keys[3 + a, 64 * k : 64 * k + 64] = rest[k, 64 * a : 64 * a + 64]
            keys[6 + a, 16 * k : 16 * k + 16] = rest[k, 192 + 16 * a : 208 + 16 * a]
            for j in range(3):
                keys[6 + a, 128 * (j + 1) + 16 * k : 128 * (j + 1) + 16 * k + 16] = thirds[j][
                    k, 16 * a : 16 * a + 16
                ]

    def position(index, a):
        o = [offs[level, 3 * where[0] + a] for level in range(3)]
        return jnp.where(
            index < 256,
            8 * index + o[0],
            jnp.where(index < 320, 32 * (index - 256) + o[1], 128 * (index - 320) + o[2]),
        )

    for a in range(3):
        base = PER_HEAD * a
        q, g = rows_of(query_first, query_rest, a), grads[base : base + PER_HEAD]
        same = jnp.where(
            position(iota((PER_HEAD, 1), 0), a) == position(iota((1, PER_HEAD), 1), a), 1.0, 0.0
        ).astype(F32)

        def over_levels(column):
            wide = jnp.broadcast_to(column, (PER_HEAD, 128))
            return jnp.dot(same, wide, precision=lax.Precision.HIGHEST, preferred_element_type=F32)[:, 0:1]

        expo = [
            jnp.exp(nt(q[low:high], keys[3 * level + a]) * SCALE) for level, (low, high) in enumerate(SPANS)
        ]
        total = over_levels(jnp.concatenate([jnp.sum(e, 1, keepdims=True) for e in expo], 0))
        inverse = 1.0 / total
        weights = [e * inverse[low:high] for e, (low, high) in zip(expo, SPANS)]
        rounded = [w.astype(BF) for w in weights]
        out = jnp.concatenate([nn(rounded[level], keys[3 * level + a]) for level in range(3)], 0)
        attended[base : base + PER_HEAD] = out.astype(BF)
        delta = over_levels(jnp.sum(g.astype(F32) * out, 1, keepdims=True))
        for level, (low, high) in enumerate(SPANS):
            block = keys[3 * level + a]
            back = nt(g[low:high], block)
            score = (weights[level] * (back - delta[low:high]) * SCALE).astype(BF)
            query_grad[base + low : base + high] = nn(score, block).astype(BF)
            pair = (tn(score, q[low:high]) + tn(rounded[level], g[low:high])).astype(BF)
            if level == 0:
                first_back[256 * a : 256 * a + 256] = pair[0:256]
                first_send[256 * a : 256 * a + 256] = pair[256:512]
            elif level == 1:
                for k in range(8):
                    second_back[k, 64 * a : 64 * a + 64] = pair[64 * k : 64 * k + 64]
            else:
                for j in range(4):
                    for k in range(8):
                        third_back[j][k, 16 * a : 16 * a + 16] = pair[128 * j + 16 * k : 128 * j + 16 * k + 16]


def put_chunks(place, held, chunks, sends):
    for c in range(64):
        chunks[c // 16, c % 16] = held[36 * c : 36 * c + 36].astype(BF)
    for k in range(4):
        sends[k][...] = chunks[place[0] ^ k]


def put_grad(held, kind, a, value):
    for b in range(6):
        start = 384 * b + 192 * kind + 64 * a
        held[start : start + 64] = value[:, 128 * b : 128 * b + 128]


def early_kernel(place, attended, query_grad, c_first, c_rest, x_first, x_rest, *refs):
    sends, held, chunks = refs[:4], refs[4], refs[5]
    for a in range(3):
        own = slice(PER_HEAD * a, PER_HEAD * a + PER_HEAD)
        put_grad(held, 0, a, tn(query_grad[own], rows_of(x_first, x_rest, a))[0:64])
        put_grad(held, 1, a, tn(attended[own], rows_of(c_first, c_rest, a))[64:128])
    put_chunks(place, held, chunks, sends)


def output_kernel(attended, w_out, s0, s1, s2, s3):
    parts = []
    for a in range(3):
        own = slice(PER_HEAD * a, PER_HEAD * a + PER_HEAD)
        parts.append(nn(attended[own], pad_out(w_out, a)).astype(BF))
    ungroup(parts, (s0, s1, s2, s3))


def total_of(parts, count):
    return functools.reduce(lambda x, y: x + y, [parts[k].astype(F32) for k in range(count)])


def third_sum_kernel(second, t0, t1, t2, t3, sends):
    for k in range(8):
        sends[k, 0:192] = second[k]
        sends[k, 192:240] = total_of([t[k] for t in (t0, t1, t2, t3)], 4).astype(BF)


def change_kernel(place, first_own, first_other, rests, query_grad, x_first, x_rest, *refs):
    sends, changes, held, chunks = refs[:4], refs[4], refs[5], refs[6]
    first = first_own[...].astype(F32) + first_other[...].astype(F32)
    rest = total_of(rests, 8)
    for a in range(3):
        own = slice(PER_HEAD * a, PER_HEAD * a + PER_HEAD)
        pair = jnp.concatenate(
            [first[256 * a : 256 * a + 256], rest[64 * a : 64 * a + 64], rest[192 + 16 * a : 208 + 16 * a]], 0
        ).astype(BF)
        made = tn(pair, rows_of(x_first, x_rest, a))
        put_grad(held, 0, a, made[0:64])
        put_grad(held, 1, a, made[64:128])
        changes[own] = jnp.concatenate([pair, query_grad[own]], 1)
    put_chunks(place, held, chunks, sends)


def input_kernel(changes, joined, s0, s1, s2, s3):
    parts = []
    for a in range(3):
        own = slice(PER_HEAD * a, PER_HEAD * a + PER_HEAD)
        parts.append(nn(changes[own], joined[256 * a : 256 * a + 256]).astype(BF))
    ungroup(parts, (s0, s1, s2, s3))


def x_sum_kernel(*refs):
    out, held = refs[8], refs[9]
    for y in range(16):
        for half in range(2):
            held[36 * half : 36 * half + 36] = total_of([part[y] for part in refs[4 * half : 4 * half + 4]], 4)
        out[y] = held[...].astype(BF)


def yz_sum_kernel(got, sends):
    total = total_of(got, 16).astype(BF)
    for y in range(16):
        sends[y] = total


def place_kernel(place, b0, b1, b2, b3, *refs):
    outs, chunks, wide, held = refs[:4], refs[4], refs[5], refs[6]
    for k, block in enumerate((b0, b1, b2, b3)):
        chunks[place[0] ^ k] = block[...]
    for c in range(64):
        wide[...] = chunks[c // 16, c % 16].astype(F32)
        for half in range(2):
            held[half, 36 * c : 36 * c + 36] = wide[36 * half : 36 * half + 36]
    for half in range(2):
        for kind in range(2):
            for b in range(6):
                start = 384 * b + 192 * kind
                outs[2 * half + kind][:, 128 * b : 128 * b + 128] = held[half, start : start + 192]


def spread_kernel(offs, where, s0, s1, s2, s3, out):
    total = None
    for k, slot in enumerate((s0, s1, s2, s3)):
        term = nn(spread_matrix(offs, where[0] ^ k), slot[...])
        total = term if total is None else total + term
    out[...] = total.astype(BF)


def swap(value, axis, k):
    count = lax.axis_size(axis)
    return lax.ppermute(value, axis, [(i, i ^ k) for i in range(count)])


def deal(value, axis):
    return lax.all_to_all(value, axis, 0, 0, tiled=True)


YZ_AXES = ("yh", "z")


def per_device(tokens, cotangent, w_query, w_key, w_value, w_out, offsets):
    where = lax.axis_index(HEAD_AXES).reshape(1).astype(jnp.int32)
    place = lax.axis_index("x").reshape(1).astype(jnp.int32)

    def picked(source, first, rest, index):
        shape = ((192 * first + 64 * rest, WIDTH), BF)
        body = functools.partial(pick_kernel, first, rest)
        flops = 8 * shape[0][0] * 512 * 768
        return list(call(body, [shape] * 4, smem=2, flops=flops)(offsets, index, source))

    def to_heads(slots):
        return [slots[0]] + [swap(slots[k], HEAD_AXES, k) for k in (1, 2, 3)]

    tie = lax.optimization_barrier
    (joined,) = call(join_kernel, [((768, WIDTH), BF)])(w_query, w_key, w_value)
    token_rest = to_heads(picked(tokens, 0, 1, where))
    token_first, grad_rows = picked(tokens, 1, 0, where), picked(cotangent, 1, 1, where)
    token_rest[2], token_rest[3], token_first = tie((token_rest[2], token_rest[3], token_first))
    token_first, grad_rows = to_heads(token_first), to_heads(grad_rows)
    token_rest, token_first[0], grad_rows[0], joined = tie((token_rest, token_first[0], grad_rows[0], joined))

    half_chunks, full_chunks = ((16, 36, 128), BF), ((16, 72, 128), BF)
    halves = [((2304, 128), F32), ((4, 16, 36, 128), BF)]
    wide, half, short = ((3 * PER_HEAD, 128), BF), ((768, 128), BF), ((240, 128), BF)
    rest_shape, second_shape, third_shape = ((8, 240, 128), BF), ((8, 192, 128), BF), ((8, 48, 128), BF)
    whole_first, whole_rest = ((768, WIDTH), BF), ((240, WIDTH), BF)
    slot = ((SLOT, WIDTH), BF)

    x_rest, query_rest, rest = call(
        project_rest_kernel, [whole_rest, short, rest_shape], flops=2 * 240 * 768 * 256
    )(*token_rest, joined)
    rest, token_first[2] = tie((rest, token_first[2]))
    rest = deal(rest, "z")
    x_first, query_first, first = call(
        project_first_kernel, [whole_first, half, half], flops=2 * 768 * 768 * 256
    )(*token_first, joined)
    first_other = swap(first, "z", 1)
    third, x_first = tie((rest[:, 192:240], x_first))
    thirds = [swap(third, "x", j) for j in (1, 2, 3)]
    c_first, c_rest, grads = call(
        grad_rows_kernel, [whole_first, whole_rest, wide], flops=2 * 1008 * 768 * 128
    )(*grad_rows, w_out)

    attended, query_grad, first_back, first_send, second_back, *third_back = call(
        attention_kernel,
        [wide, wide, half, half, second_shape] + [third_shape] * 4,
        scratch=[((9, 512, 128), BF)],
        smem=2,
        flops=2 * 1008 * 512 * 128 * 7,
    )(offsets, where, query_first, query_rest, grads, first, first_other, rest, *thirds)

    third_got = [third_back[0]] + [swap(third_back[j], "x", j) for j in (1, 2, 3)]
    first_got = swap(first_send, "z", 1)
    early = call(early_kernel, [half_chunks] * 4, scratch=halves, smem=1, flops=4 * 1008 * 768 * 128)(
        place, attended, query_grad, c_first, c_rest, x_first, x_rest
    )
    mixed_slots = call(output_kernel, [slot] * 4, flops=2 * 1008 * 768 * 128)(attended, w_out)
    mixed_slots = to_heads(mixed_slots)
    early = [early[0]] + [swap(early[k], "x", k) for k in (1, 2, 3)]
    third_got, first_got, mixed_slots[0], early[0] = tie((third_got, first_got, mixed_slots[0], early[0]))
    (rest_back,) = call(third_sum_kernel, [rest_shape])(second_back, *third_got)
    rest_got = deal(rest_back, "z")
    rest_got, early = tie((rest_got, early))

    *late, changes = call(
        change_kernel,
        [half_chunks] * 4 + [((3 * PER_HEAD, 256), BF)],
        scratch=halves,
        smem=1,
        flops=2 * 1008 * 768 * 128,
    )(place, first_back, first_got, rest_got, query_grad, x_first, x_rest)
    late = [late[0]] + [swap(late[k], "x", k) for k in (1, 2, 3)]
    change_slots = call(input_kernel, [slot] * 4, flops=2 * 1008 * 768 * 256)(changes, joined)
    spread = call(spread_kernel, [((ROWS, WIDTH), BF)], smem=2, flops=2 * 1024 * 512 * 768)
    (mixed,) = spread(offsets, where, *mixed_slots)
    (parts,) = call(x_sum_kernel, [full_chunks], scratch=[((72, 128), F32)])(*early, *late)
    (part,) = call(yz_sum_kernel, [full_chunks])(deal(parts, YZ_AXES))
    part, mixed, change_slots = tie((part, mixed, change_slots))
    block, change_slots = deal(part, YZ_AXES), to_heads(change_slots)
    blocks = [block] + [swap(block, "x", k) for k in (1, 2, 3)]
    (grad_tokens,) = spread(offsets, where, *change_slots)
    grad_query, grad_out, grad_key, grad_value = call(
        place_kernel,
        [((192, WIDTH), F32)] * 4,
        scratch=[((4, 16, 72, 128), BF), ((72, 128), F32), ((2, 2304, 128), F32)],
        smem=1,
    )(place, *blocks)
    return mixed, grad_tokens, grad_query, grad_key, grad_value, grad_out


def solution(mesh):
    fine = jax.sharding.Mesh(mesh.devices.reshape(2, 4, 8, 2, 2), ("yh", "x", "z", "yl", "core"))
    rows = P(("yh", "x", "z", "yl", "core"), None)
    cut = P(HEAD_AXES, None)
    return jax.shard_map(
        per_device,
        mesh=fine,
        in_specs=(rows, rows, cut, cut, cut, cut, P()),
        out_specs=(rows, rows, cut, cut, cut, cut),
        check_vma=False,
    )
```

```python
import functools

import jax
import jax.numpy as jnp
from jax import lax
from jax.experimental import pallas as pl
from jax.experimental.pallas import tpu as pltpu
from jax.sharding import PartitionSpec as P

BF = jnp.bfloat16
F32 = jnp.float32
WIDTH = 768
ROWS = 512
SLOT = 256
PER_HEAD = 336
SPANS = ((0, 256), (256, 320), (320, 336))
SCALE = 0.125
HEAD_AXES = ("yl", "core")


def nn(a, b):
    return jnp.dot(a, b, preferred_element_type=F32)


def nt(a, b):
    return lax.dot_general(a, b, (((1,), (1,)), ((), ())), preferred_element_type=F32)


def tn(a, b):
    return lax.dot_general(a, b, (((0,), (0,)), ((), ())), preferred_element_type=F32)


def iota(shape, dim):
    return lax.broadcasted_iota(jnp.int32, shape, dim)


def ones_where(mask):
    return jnp.where(mask, 1.0, 0.0).astype(BF)


def pick_first(offs, group):
    row, col = iota((64, ROWS), 0), iota((64, ROWS), 1)
    return jnp.concatenate([ones_where(8 * row + offs[0, 3 * group + a] == col) for a in range(3)], 0)


def pick_rest(offs, group):
    row, col = iota((16, ROWS), 0), iota((16, ROWS), 1)
    parts = [ones_where(32 * row + offs[1, 3 * group + a] == col) for a in range(3)]
    third = [offs[2, 3 * group + a] for a in range(3)]
    off = jnp.where(row < 4, third[0], jnp.where(row < 8, third[1], jnp.where(row < 12, third[2], 4 * ROWS)))
    parts.append(ones_where(128 * (row & 3) + off == col))
    return jnp.concatenate(parts, 0)


def spread_matrix(offs, group):
    lane = iota((1, SLOT), 1)
    o = [[offs[level, 3 * group + a] for a in range(3)] for level in range(3)]
    first = 8 * (lane & 63) + jnp.where(lane < 64, o[0][0], jnp.where(lane < 128, o[0][1], o[0][2]))
    second = 32 * (lane & 15) + jnp.where(lane < 208, o[1][0], jnp.where(lane < 224, o[1][1], o[1][2]))
    third = 128 * (lane & 3) + jnp.where(
        lane < 244, o[2][0], jnp.where(lane < 248, o[2][1], jnp.where(lane < 252, o[2][2], 4 * ROWS))
    )
    pos = jnp.where(lane < 192, first, jnp.where(lane < 240, second, third))
    return ones_where(iota((ROWS, SLOT), 0) == pos)


def third_order(dim):
    new, old = iota((64, 64), dim), iota((64, 64), 1 - dim)
    source = 16 * ((new >> 2) & 3) + 4 * (new >> 4) + (new & 3)
    return ones_where((source == old) & (new < 48))


def call(body, outs, scratch=(), smem=0, flops=0, nbytes=4 << 20):
    def run(*args):
        vmem = pl.BlockSpec(memory_space=pltpu.VMEM)
        specs = [pl.BlockSpec(memory_space=pltpu.SMEM)] * smem + [vmem] * (len(args) - smem)
        return pl.pallas_call(
            body,
            out_shape=tuple(jax.ShapeDtypeStruct(shape, kind) for shape, kind in outs),
            in_specs=specs,
            out_specs=tuple(vmem for _ in outs),
            scratch_shapes=[pltpu.VMEM(shape, kind) for shape, kind in scratch],
            compiler_params=pltpu.CompilerParams(vmem_limit_bytes=40 << 20),
            cost_estimate=pl.CostEstimate(flops=flops, bytes_accessed=nbytes, transcendentals=0),
        )(*args)

    return run


def pick_kernel(first, rest, offs, where, source, *outs):
    for k in (2, 3, 1, 0):
        group = where[0] ^ k
        parts = ([pick_first(offs, group)] if first else []) + ([pick_rest(offs, group)] if rest else [])
        outs[k][...] = nn(jnp.concatenate(parts, 0), source[...]).astype(BF)


def regroup_rest(rests, whole):
    third = jnp.concatenate([rest[48:64] for rest in rests], 0)
    third = nn(third_order(0), third).astype(BF)
    for a in range(3):
        for k in range(4):
            whole[80 * a + 16 * k : 80 * a + 16 * k + 16] = rests[k][16 * a : 16 * a + 16]
        whole[80 * a + 64 : 80 * a + 80] = third[16 * a : 16 * a + 16]


def regroup_first(firsts, whole):
    for a in range(3):
        for k in range(4):
            whole[256 * a + 64 * k : 256 * a + 64 * k + 64] = firsts[k][64 * a : 64 * a + 64]


def ungroup(parts, slots):
    third = jnp.concatenate([part[320:336] for part in parts] + [jnp.zeros((16, WIDTH), BF)], 0)
    third = nn(third_order(1), third).astype(BF)
    for k in range(4):
        for a in range(3):
            slots[k][64 * a : 64 * a + 64] = parts[a][64 * k : 64 * k + 64]
            slots[k][192 + 16 * a : 208 + 16 * a] = parts[a][256 + 16 * k : 272 + 16 * k]
        slots[k][240:256] = third[16 * k : 16 * k + 16]


def join_kernel(w_query, w_key, w_value, joined):
    for a in range(3):
        own = slice(64 * a, 64 * a + 64)
        joined[256 * a : 256 * a + 64] = w_key[own]
        joined[256 * a + 64 : 256 * a + 128] = w_value[own]
        joined[256 * a + 128 : 256 * a + 192] = w_query[own]
        joined[256 * a + 192 : 256 * a + 256] = jnp.zeros((64, WIDTH), BF)


def pad_out(w_out, a):
    return jnp.concatenate([jnp.zeros((64, WIDTH), BF), w_out[64 * a : 64 * a + 64]], 0)


def project_rest_kernel(x0, x1, x2, x3, joined, whole, query, rest):
    regroup_rest((x0, x1, x2, x3), whole)
    for a in range(3):
        made = nt(whole[80 * a : 80 * a + 80], joined[256 * a : 256 * a + 256]).astype(BF)
        query[80 * a : 80 * a + 80] = made[:, 128:256]
        for k in range(8):
            rest[k, 64 * a : 64 * a + 64] = made[0:64, 0:128]
            rest[k, 192 + 16 * a : 208 + 16 * a] = made[64:80, 0:128]


def project_first_kernel(x0, x1, x2, x3, joined, whole, query, first):
    regroup_first((x0, x1, x2, x3), whole)
    for a in range(3):
        own = slice(256 * a, 256 * a + 256)
        made = nt(whole[own], joined[own]).astype(BF)
        query[own] = made[:, 128:256]
        first[own] = made[:, 0:128]


def rows_of(first, rest, a):
    return jnp.concatenate([first[256 * a : 256 * a + 256], rest[80 * a : 80 * a + 80]], 0)


def grad_rows_kernel(c0, c1, c2, c3, w_out, whole_first, whole_rest, grads):
    slots = (c0, c1, c2, c3)
    regroup_first(slots, whole_first)
    regroup_rest([slot.at[192:256] for slot in slots], whole_rest)
    for a in range(3):
        base = PER_HEAD * a
        grads[base : base + PER_HEAD] = nt(rows_of(whole_first, whole_rest, a), pad_out(w_out, a)).astype(BF)


def attention_kernel(offs, where, query_first, query_rest, grads, first_own, first_other, rest, *refs):
    thirds = refs[:3]
    attended, query_grad, first_back, first_send, second_back = refs[3:8]
    third_back, keys = refs[8:12], refs[12]
    for a in range(3):
        keys[a, 0:256] = first_own[256 * a : 256 * a + 256]
        keys[a, 256:512] = first_other[256 * a : 256 * a + 256]
        for k in range(8):
            keys[3 + a, 64 * k : 64 * k + 64] = rest[k, 64 * a : 64 * a + 64]
            keys[6 + a, 16 * k : 16 * k + 16] = rest[k, 192 + 16 * a : 208 + 16 * a]
            for j in range(3):
                keys[6 + a, 128 * (j + 1) + 16 * k : 128 * (j + 1) + 16 * k + 16] = thirds[j][
                    k, 16 * a : 16 * a + 16
                ]

    def position(index, a):
        o = [offs[level, 3 * where[0] + a] for level in range(3)]
        return jnp.where(
            index < 256,
            8 * index + o[0],
            jnp.where(index < 320, 32 * (index - 256) + o[1], 128 * (index - 320) + o[2]),
        )

    for a in range(3):
        base = PER_HEAD * a
        q, g = rows_of(query_first, query_rest, a), grads[base : base + PER_HEAD]
        same = jnp.where(
            position(iota((PER_HEAD, 1), 0), a) == position(iota((1, PER_HEAD), 1), a), 1.0, 0.0
        ).astype(F32)

        def over_levels(column):
            wide = jnp.broadcast_to(column, (PER_HEAD, 128))
            return jnp.dot(same, wide, precision=lax.Precision.HIGHEST, preferred_element_type=F32)[:, 0:1]

        expo = [
            jnp.exp(nt(q[low:high], keys[3 * level + a]) * SCALE) for level, (low, high) in enumerate(SPANS)
        ]
        total = over_levels(jnp.concatenate([jnp.sum(e, 1, keepdims=True) for e in expo], 0))
        inverse = 1.0 / total
        weights = [e * inverse[low:high] for e, (low, high) in zip(expo, SPANS)]
        rounded = [w.astype(BF) for w in weights]
        out = jnp.concatenate([nn(rounded[level], keys[3 * level + a]) for level in range(3)], 0)
        attended[base : base + PER_HEAD] = out.astype(BF)
        delta = over_levels(jnp.sum(g.astype(F32) * out, 1, keepdims=True))
        for level, (low, high) in enumerate(SPANS):
            block = keys[3 * level + a]
            back = nt(g[low:high], block)
            score = (weights[level] * (back - delta[low:high]) * SCALE).astype(BF)
            query_grad[base + low : base + high] = nn(score, block).astype(BF)
            pair = (tn(score, q[low:high]) + tn(rounded[level], g[low:high])).astype(BF)
            if level == 0:
                first_back[256 * a : 256 * a + 256] = pair[0:256]
                first_send[256 * a : 256 * a + 256] = pair[256:512]
            elif level == 1:
                for k in range(8):
                    second_back[k, 64 * a : 64 * a + 64] = pair[64 * k : 64 * k + 64]
            else:
                for j in range(4):
                    for k in range(8):
                        third_back[j][k, 16 * a : 16 * a + 16] = pair[128 * j + 16 * k : 128 * j + 16 * k + 16]


def put_chunks(place, held, chunks, sends):
    for c in range(64):
        chunks[c // 16, c % 16] = held[36 * c : 36 * c + 36].astype(BF)
    for k in range(4):
        sends[k][...] = chunks[place[1] ^ k]


def put_grad(held, kind, a, value):
    for b in range(6):
        start = 384 * b + 192 * kind + 64 * a
        held[start : start + 64] = value[:, 128 * b : 128 * b + 128]


def early_kernel(place, attended, query_grad, c_first, c_rest, x_first, x_rest, *refs):
    sends, held, chunks = refs[:4], refs[4], refs[5]
    for a in range(3):
        own = slice(PER_HEAD * a, PER_HEAD * a + PER_HEAD)
        put_grad(held, 0, a, tn(query_grad[own], rows_of(x_first, x_rest, a))[0:64])
        put_grad(held, 1, a, tn(attended[own], rows_of(c_first, c_rest, a))[64:128])
    put_chunks(place, held, chunks, sends)


def output_kernel(attended, w_out, s0, s1, s2, s3):
    parts = []
    for a in range(3):
        own = slice(PER_HEAD * a, PER_HEAD * a + PER_HEAD)
        parts.append(nn(attended[own], pad_out(w_out, a)).astype(BF))
    ungroup(parts, (s0, s1, s2, s3))


def total_of(parts, count):
    return functools.reduce(lambda x, y: x + y, [parts[k].astype(F32) for k in range(count)])


def third_sum_kernel(second, t0, t1, t2, t3, sends):
    for k in range(8):
        sends[k, 0:192] = second[k]
        sends[k, 192:240] = total_of([t[k] for t in (t0, t1, t2, t3)], 4).astype(BF)


def change_kernel(place, first_own, first_other, rests, query_grad, x_first, x_rest, *refs):
    sends, changes, held, chunks = refs[:4], refs[4], refs[5], refs[6]
    first = first_own[...].astype(F32) + first_other[...].astype(F32)
    rest = total_of(rests, 8)
    for a in range(3):
        own = slice(PER_HEAD * a, PER_HEAD * a + PER_HEAD)
        pair = jnp.concatenate(
            [first[256 * a : 256 * a + 256], rest[64 * a : 64 * a + 64], rest[192 + 16 * a : 208 + 16 * a]], 0
        ).astype(BF)
        made = tn(pair, rows_of(x_first, x_rest, a))
        put_grad(held, 0, a, made[0:64])
        put_grad(held, 1, a, made[64:128])
        changes[own] = jnp.concatenate([pair, query_grad[own]], 1)
    put_chunks(place, held, chunks, sends)


def input_kernel(changes, joined, s0, s1, s2, s3):
    parts = []
    for a in range(3):
        own = slice(PER_HEAD * a, PER_HEAD * a + PER_HEAD)
        parts.append(nn(changes[own], joined[256 * a : 256 * a + 256]).astype(BF))
    ungroup(parts, (s0, s1, s2, s3))


def x_sum_kernel(*refs):
    out, held = refs[8], refs[9]
    for y in range(16):
        for half in range(2):
            held[36 * half : 36 * half + 36] = total_of([part[y] for part in refs[4 * half : 4 * half + 4]], 4)
        out[y] = held[...].astype(BF)


def yz_sum_kernel(got, sends):
    total = total_of(got, 16).astype(BF)
    for y in range(16):
        sends[y] = total


def place_kernel(place, b0, b1, b2, b3, *refs):
    outs, chunks, wide, held = refs[:4], refs[4], refs[5], refs[6]
    for k, block in enumerate((b0, b1, b2, b3)):
        chunks[place[1] ^ k] = block[...]
    for c in range(64):
        wide[...] = chunks[c // 16, c % 16].astype(F32)
        for half in range(2):
            held[half, 36 * c : 36 * c + 36] = wide[36 * half : 36 * half + 36]
    for half in range(2):
        for kind in range(2):
            for b in range(6):
                start = 384 * b + 192 * kind
                outs[2 * half + kind][:, 128 * b : 128 * b + 128] = held[half, start : start + 192]


def spread_kernel(offs, where, s0, s1, s2, s3, out):
    total = None
    for k, slot in enumerate((s0, s1, s2, s3)):
        term = nn(spread_matrix(offs, where[0] ^ k), slot[...])
        total = term if total is None else total + term
    out[...] = total.astype(BF)


def swap(value, axis, k):
    count = lax.axis_size(axis)
    return lax.ppermute(value, axis, [(i, i ^ k) for i in range(count)])


def deal(value, axis):
    return lax.all_to_all(value, axis, 0, 0, tiled=True)


YZ_AXES = ("yh", "z")


def per_device(tokens, cotangent, w_query, w_key, w_value, w_out, offsets):
    where = jnp.stack([lax.axis_index(HEAD_AXES), lax.axis_index("x")]).astype(jnp.int32)

    def picked(source, first, rest, index):
        shape = ((192 * first + 64 * rest, WIDTH), BF)
        body = functools.partial(pick_kernel, first, rest)
        flops = 8 * shape[0][0] * 512 * 768
        return list(call(body, [shape] * 4, smem=2, flops=flops)(offsets, index, source))

    def to_heads(slots):
        return [slots[0]] + [swap(slots[k], HEAD_AXES, k) for k in (1, 2, 3)]

    tie = lax.optimization_barrier
    (joined,) = call(join_kernel, [((768, WIDTH), BF)])(w_query, w_key, w_value)
    token_rest = to_heads(picked(tokens, 0, 1, where))
    token_first, grad_rows = picked(tokens, 1, 0, where), picked(cotangent, 1, 1, where)
    token_rest[2], token_rest[3], token_first = tie((token_rest[2], token_rest[3], token_first))
    token_first, grad_rows = to_heads(token_first), to_heads(grad_rows)
    token_rest, token_first[0], grad_rows[0], joined = tie((token_rest, token_first[0], grad_rows[0], joined))

    half_chunks, full_chunks = ((16, 36, 128), BF), ((16, 72, 128), BF)
    halves = [((2304, 128), F32), ((4, 16, 36, 128), BF)]
    wide, half, short = ((3 * PER_HEAD, 128), BF), ((768, 128), BF), ((240, 128), BF)
    rest_shape, second_shape, third_shape = ((8, 240, 128), BF), ((8, 192, 128), BF), ((8, 48, 128), BF)
    whole_first, whole_rest = ((768, WIDTH), BF), ((240, WIDTH), BF)
    slot = ((SLOT, WIDTH), BF)

    x_rest, query_rest, rest = call(
        project_rest_kernel, [whole_rest, short, rest_shape], flops=2 * 240 * 768 * 256
    )(*token_rest, joined)
    rest, token_first[2] = tie((rest, token_first[2]))
    rest = deal(rest, "z")
    x_first, query_first, first = call(
        project_first_kernel, [whole_first, half, half], flops=2 * 768 * 768 * 256
    )(*token_first, joined)
    first_other = swap(first, "z", 1)
    third, x_first = tie((rest[:, 192:240], x_first))
    thirds = [swap(third, "x", j) for j in (1, 2, 3)]
    c_first, c_rest, grads = call(
        grad_rows_kernel, [whole_first, whole_rest, wide], flops=2 * 1008 * 768 * 128
    )(*grad_rows, w_out)

    attended, query_grad, first_back, first_send, second_back, *third_back = call(
        attention_kernel,
        [wide, wide, half, half, second_shape] + [third_shape] * 4,
        scratch=[((9, 512, 128), BF)],
        smem=2,
        flops=2 * 1008 * 512 * 128 * 7,
    )(offsets, where, query_first, query_rest, grads, first, first_other, rest, *thirds)

    third_got = [third_back[0]] + [swap(third_back[j], "x", j) for j in (1, 2, 3)]
    first_got = swap(first_send, "z", 1)
    early = call(early_kernel, [half_chunks] * 4, scratch=halves, smem=1, flops=4 * 1008 * 768 * 128)(
        where, attended, query_grad, c_first, c_rest, x_first, x_rest
    )
    mixed_slots = call(output_kernel, [slot] * 4, flops=2 * 1008 * 768 * 128)(attended, w_out)
    mixed_slots = to_heads(mixed_slots)
    early = [early[0]] + [swap(early[k], "x", k) for k in (1, 2, 3)]
    third_got, first_got, mixed_slots[0], early[0] = tie((third_got, first_got, mixed_slots[0], early[0]))
    (rest_back,) = call(third_sum_kernel, [rest_shape])(second_back, *third_got)
    rest_got = deal(rest_back, "z")
    rest_got, early, mixed_slots = tie((rest_got, early, mixed_slots))

    *late, changes = call(
        change_kernel,
        [half_chunks] * 4 + [((3 * PER_HEAD, 256), BF)],
        scratch=halves,
        smem=1,
        flops=2 * 1008 * 768 * 128,
    )(where, first_back, first_got, rest_got, query_grad, x_first, x_rest)
    late = [late[0]] + [swap(late[k], "x", k) for k in (1, 2, 3)]
    change_slots = call(input_kernel, [slot] * 4, flops=2 * 1008 * 768 * 256)(changes, joined)
    spread = call(spread_kernel, [((ROWS, WIDTH), BF)], smem=2, flops=2 * 1024 * 512 * 768)
    (mixed,) = spread(offsets, where, *mixed_slots)
    (parts,) = call(x_sum_kernel, [full_chunks], scratch=[((72, 128), F32)])(*early, *late)
    (part,) = call(yz_sum_kernel, [full_chunks])(deal(parts, YZ_AXES))
    part, mixed, change_slots = tie((part, mixed, change_slots))
    block, change_slots = deal(part, YZ_AXES), to_heads(change_slots)
    blocks = [block] + [swap(block, "x", k) for k in (1, 2, 3)]
    (grad_tokens,) = spread(offsets, where, *change_slots)
    grad_query, grad_out, grad_key, grad_value = call(
        place_kernel,
        [((192, WIDTH), F32)] * 4,
        scratch=[((4, 16, 72, 128), BF), ((72, 128), F32), ((2, 2304, 128), F32)],
        smem=1,
    )(where, *blocks)
    return mixed, grad_tokens, grad_query, grad_key, grad_value, grad_out


def solution(mesh):
    fine = jax.sharding.Mesh(mesh.devices.reshape(2, 4, 8, 2, 2), ("yh", "x", "z", "yl", "core"))
    rows = P(("yh", "x", "z", "yl", "core"), None)
    cut = P(HEAD_AXES, None)
    return jax.shard_map(
        per_device,
        mesh=fine,
        in_specs=(rows, rows, cut, cut, cut, cut, P()),
        out_specs=(rows, rows, cut, cut, cut, cut),
        check_vma=False,
    )
```

```python
import functools

import jax
import jax.numpy as jnp
from jax import lax
from jax.experimental import pallas as pl
from jax.experimental.pallas import tpu as pltpu
from jax.sharding import PartitionSpec as P

BF = jnp.bfloat16
F32 = jnp.float32
WIDTH = 768
ROWS = 512
SLOT = 256
PER_HEAD = 336
SPANS = ((0, 256), (256, 320), (320, 336))
SCALE = 0.125
HEAD_AXES = ("yl", "core")


def nn(a, b):
    return jnp.dot(a, b, preferred_element_type=F32)


def nt(a, b):
    return lax.dot_general(a, b, (((1,), (1,)), ((), ())), preferred_element_type=F32)


def tn(a, b):
    return lax.dot_general(a, b, (((0,), (0,)), ((), ())), preferred_element_type=F32)


def iota(shape, dim):
    return lax.broadcasted_iota(jnp.int32, shape, dim)


def ones_where(mask):
    return jnp.where(mask, 1.0, 0.0).astype(BF)


def pick_first(offs, group):
    row, col = iota((64, ROWS), 0), iota((64, ROWS), 1)
    return jnp.concatenate([ones_where(8 * row + offs[0, 3 * group + a] == col) for a in range(3)], 0)


def pick_rest(offs, group):
    row, col = iota((16, ROWS), 0), iota((16, ROWS), 1)
    parts = [ones_where(32 * row + offs[1, 3 * group + a] == col) for a in range(3)]
    third = [offs[2, 3 * group + a] for a in range(3)]
    off = jnp.where(row < 4, third[0], jnp.where(row < 8, third[1], jnp.where(row < 12, third[2], 4 * ROWS)))
    parts.append(ones_where(128 * (row & 3) + off == col))
    return jnp.concatenate(parts, 0)


def spread_matrix(offs, group):
    lane = iota((1, SLOT), 1)
    o = [[offs[level, 3 * group + a] for a in range(3)] for level in range(3)]
    first = 8 * (lane & 63) + jnp.where(lane < 64, o[0][0], jnp.where(lane < 128, o[0][1], o[0][2]))
    second = 32 * (lane & 15) + jnp.where(lane < 208, o[1][0], jnp.where(lane < 224, o[1][1], o[1][2]))
    third = 128 * (lane & 3) + jnp.where(
        lane < 244, o[2][0], jnp.where(lane < 248, o[2][1], jnp.where(lane < 252, o[2][2], 4 * ROWS))
    )
    pos = jnp.where(lane < 192, first, jnp.where(lane < 240, second, third))
    return ones_where(iota((ROWS, SLOT), 0) == pos)


def third_order(dim):
    new, old = iota((64, 64), dim), iota((64, 64), 1 - dim)
    source = 16 * ((new >> 2) & 3) + 4 * (new >> 4) + (new & 3)
    return ones_where((source == old) & (new < 48))


def call(body, outs, scratch=(), smem=0, flops=0, nbytes=4 << 20):
    def run(*args):
        vmem = pl.BlockSpec(memory_space=pltpu.VMEM)
        specs = [pl.BlockSpec(memory_space=pltpu.SMEM)] * smem + [vmem] * (len(args) - smem)
        return pl.pallas_call(
            body,
            out_shape=tuple(jax.ShapeDtypeStruct(shape, kind) for shape, kind in outs),
            in_specs=specs,
            out_specs=tuple(vmem for _ in outs),
            scratch_shapes=[pltpu.VMEM(shape, kind) for shape, kind in scratch],
            compiler_params=pltpu.CompilerParams(vmem_limit_bytes=40 << 20),
            cost_estimate=pl.CostEstimate(flops=flops, bytes_accessed=nbytes, transcendentals=0),
        )(*args)

    return run


def pick_kernel(first, rest, offs, where, source, *outs):
    for k in (2, 3, 1, 0):
        group = where[0] ^ k
        parts = ([pick_first(offs, group)] if first else []) + ([pick_rest(offs, group)] if rest else [])
        outs[k][...] = nn(jnp.concatenate(parts, 0), source[...]).astype(BF)


def regroup_rest(rests, whole):
    third = jnp.concatenate([rest[48:64] for rest in rests], 0)
    third = nn(third_order(0), third).astype(BF)
    for a in range(3):
        for k in range(4):
            whole[80 * a + 16 * k : 80 * a + 16 * k + 16] = rests[k][16 * a : 16 * a + 16]
        whole[80 * a + 64 : 80 * a + 80] = third[16 * a : 16 * a + 16]


def regroup_first(firsts, whole):
    for a in range(3):
        for k in range(4):
            whole[256 * a + 64 * k : 256 * a + 64 * k + 64] = firsts[k][64 * a : 64 * a + 64]


def ungroup(parts, slots):
    third = jnp.concatenate([part[320:336] for part in parts] + [jnp.zeros((16, WIDTH), BF)], 0)
    third = nn(third_order(1), third).astype(BF)
    for k in range(4):
        for a in range(3):
            slots[k][64 * a : 64 * a + 64] = parts[a][64 * k : 64 * k + 64]
            slots[k][192 + 16 * a : 208 + 16 * a] = parts[a][256 + 16 * k : 272 + 16 * k]
        slots[k][240:256] = third[16 * k : 16 * k + 16]


def join_kernel(w_query, w_key, w_value, joined):
    for a in range(3):
        own = slice(64 * a, 64 * a + 64)
        joined[256 * a : 256 * a + 64] = w_key[own]
        joined[256 * a + 64 : 256 * a + 128] = w_value[own]
        joined[256 * a + 128 : 256 * a + 192] = w_query[own]
        joined[256 * a + 192 : 256 * a + 256] = jnp.zeros((64, WIDTH), BF)


def pad_out(w_out, a):
    return jnp.concatenate([jnp.zeros((64, WIDTH), BF), w_out[64 * a : 64 * a + 64]], 0)


def project_rest_kernel(x0, x1, x2, x3, joined, whole, query, rest):
    regroup_rest((x0, x1, x2, x3), whole)
    for a in range(3):
        made = nt(whole[80 * a : 80 * a + 80], joined[256 * a : 256 * a + 256]).astype(BF)
        query[80 * a : 80 * a + 80] = made[:, 128:256]
        for k in range(8):
            rest[k, 64 * a : 64 * a + 64] = made[0:64, 0:128]
            rest[k, 192 + 16 * a : 208 + 16 * a] = made[64:80, 0:128]


def project_first_kernel(x0, x1, x2, x3, joined, whole, query, first):
    regroup_first((x0, x1, x2, x3), whole)
    for a in range(3):
        own = slice(256 * a, 256 * a + 256)
        made = nt(whole[own], joined[own]).astype(BF)
        query[own] = made[:, 128:256]
        first[own] = made[:, 0:128]


def rows_of(first, rest, a):
    return jnp.concatenate([first[256 * a : 256 * a + 256], rest[80 * a : 80 * a + 80]], 0)


def grad_rows_kernel(c0, c1, c2, c3, w_out, whole_first, whole_rest, grads):
    slots = (c0, c1, c2, c3)
    regroup_first(slots, whole_first)
    regroup_rest([slot.at[192:256] for slot in slots], whole_rest)
    for a in range(3):
        base = PER_HEAD * a
        grads[base : base + PER_HEAD] = nt(rows_of(whole_first, whole_rest, a), pad_out(w_out, a)).astype(BF)


def attention_kernel(offs, where, query_first, query_rest, grads, first_own, first_other, rest, *refs):
    thirds = refs[:3]
    attended, query_grad, first_back, first_send, second_back = refs[3:8]
    third_back, keys = refs[8:12], refs[12]
    for a in range(3):
        keys[a, 0:256] = first_own[256 * a : 256 * a + 256]
        keys[a, 256:512] = first_other[256 * a : 256 * a + 256]
        for k in range(8):
            keys[3 + a, 64 * k : 64 * k + 64] = rest[k, 64 * a : 64 * a + 64]
            keys[6 + a, 16 * k : 16 * k + 16] = rest[k, 192 + 16 * a : 208 + 16 * a]
            for j in range(3):
                keys[6 + a, 128 * (j + 1) + 16 * k : 128 * (j + 1) + 16 * k + 16] = thirds[j][
                    k, 16 * a : 16 * a + 16
                ]

    def position(index, a):
        o = [offs[level, 3 * where[0] + a] for level in range(3)]
        return jnp.where(
            index < 256,
            8 * index + o[0],
            jnp.where(index < 320, 32 * (index - 256) + o[1], 128 * (index - 320) + o[2]),
        )

    for a in range(3):
        base = PER_HEAD * a
        q, g = rows_of(query_first, query_rest, a), grads[base : base + PER_HEAD]
        same = ones_where(position(iota((PER_HEAD, 1), 0), a) == position(iota((1, PER_HEAD), 1), a))

        def over_levels(column):
            high = column.astype(BF).astype(F32)
            middle = (column - high).astype(BF).astype(F32)
            lane = iota((PER_HEAD, 128), 1)
            parts = jnp.where(
                lane == 0, high, jnp.where(lane == 1, middle, jnp.where(lane == 2, column - high - middle, 0.0))
            )
            return jnp.sum(nn(same, parts.astype(BF)), 1, keepdims=True)

        expo = [
            jnp.exp(nt(q[low:high], keys[3 * level + a]) * SCALE) for level, (low, high) in enumerate(SPANS)
        ]
        total = over_levels(jnp.concatenate([jnp.sum(e, 1, keepdims=True) for e in expo], 0))
        inverse = 1.0 / total
        weights = [e * inverse[low:high] for e, (low, high) in zip(expo, SPANS)]
        rounded = [w.astype(BF) for w in weights]
        out = jnp.concatenate([nn(rounded[level], keys[3 * level + a]) for level in range(3)], 0)
        attended[base : base + PER_HEAD] = out.astype(BF)
        delta = over_levels(jnp.sum(g.astype(F32) * out, 1, keepdims=True))
        for level, (low, high) in enumerate(SPANS):
            block = keys[3 * level + a]
            back = nt(g[low:high], block)
            score = (weights[level] * (back - delta[low:high]) * SCALE).astype(BF)
            query_grad[base + low : base + high] = nn(score, block).astype(BF)
            pair = (tn(score, q[low:high]) + tn(rounded[level], g[low:high])).astype(BF)
            if level == 0:
                first_back[256 * a : 256 * a + 256] = pair[0:256]
                first_send[256 * a : 256 * a + 256] = pair[256:512]
            elif level == 1:
                for k in range(8):
                    second_back[k, 64 * a : 64 * a + 64] = pair[64 * k : 64 * k + 64]
            else:
                for j in range(4):
                    for k in range(8):
                        third_back[j][k, 16 * a : 16 * a + 16] = pair[128 * j + 16 * k : 128 * j + 16 * k + 16]


def put_chunks(place, held, chunks, sends):
    for c in range(64):
        chunks[c // 16, c % 16] = held[36 * c : 36 * c + 36].astype(BF)
    for k in range(4):
        sends[k][...] = chunks[place[1] ^ k]


def put_grad(held, kind, a, value):
    for b in range(6):
        start = 384 * b + 192 * kind + 64 * a
        held[start : start + 64] = value[:, 128 * b : 128 * b + 128]


def early_kernel(place, attended, query_grad, c_first, c_rest, x_first, x_rest, *refs):
    sends, held, chunks = refs[:4], refs[4], refs[5]
    for a in range(3):
        own = slice(PER_HEAD * a, PER_HEAD * a + PER_HEAD)
        put_grad(held, 0, a, tn(query_grad[own], rows_of(x_first, x_rest, a))[0:64])
        put_grad(held, 1, a, tn(attended[own], rows_of(c_first, c_rest, a))[64:128])
    put_chunks(place, held, chunks, sends)


def output_kernel(attended, w_out, s0, s1, s2, s3):
    parts = []
    for a in range(3):
        own = slice(PER_HEAD * a, PER_HEAD * a + PER_HEAD)
        parts.append(nn(attended[own], pad_out(w_out, a)).astype(BF))
    ungroup(parts, (s0, s1, s2, s3))


def total_of(parts, count):
    return functools.reduce(lambda x, y: x + y, [parts[k].astype(F32) for k in range(count)])


def third_sum_kernel(second, t0, t1, t2, t3, sends):
    for k in range(8):
        sends[k, 0:192] = second[k]
        sends[k, 192:240] = total_of([t[k] for t in (t0, t1, t2, t3)], 4).astype(BF)


def change_kernel(place, first_own, first_other, rests, query_grad, x_first, x_rest, *refs):
    sends, changes, held, chunks = refs[:4], refs[4], refs[5], refs[6]
    first = first_own[...].astype(F32) + first_other[...].astype(F32)
    rest = total_of(rests, 8)
    for a in range(3):
        own = slice(PER_HEAD * a, PER_HEAD * a + PER_HEAD)
        pair = jnp.concatenate(
            [first[256 * a : 256 * a + 256], rest[64 * a : 64 * a + 64], rest[192 + 16 * a : 208 + 16 * a]], 0
        ).astype(BF)
        made = tn(pair, rows_of(x_first, x_rest, a))
        put_grad(held, 0, a, made[0:64])
        put_grad(held, 1, a, made[64:128])
        changes[own] = jnp.concatenate([pair, query_grad[own]], 1)
    put_chunks(place, held, chunks, sends)


def input_kernel(changes, joined, s0, s1, s2, s3):
    parts = []
    for a in range(3):
        own = slice(PER_HEAD * a, PER_HEAD * a + PER_HEAD)
        parts.append(nn(changes[own], joined[256 * a : 256 * a + 256]).astype(BF))
    ungroup(parts, (s0, s1, s2, s3))


def x_sum_kernel(*refs):
    out, held = refs[8], refs[9]
    for y in range(16):
        for half in range(2):
            held[36 * half : 36 * half + 36] = total_of([part[y] for part in refs[4 * half : 4 * half + 4]], 4)
        out[y] = held[...].astype(BF)


def yz_sum_kernel(got, sends):
    total = total_of(got, 16).astype(BF)
    for y in range(16):
        sends[y] = total


def place_kernel(place, b0, b1, b2, b3, *refs):
    outs, chunks, wide, held = refs[:4], refs[4], refs[5], refs[6]
    for k, block in enumerate((b0, b1, b2, b3)):
        chunks[place[1] ^ k] = block[...]
    for c in range(64):
        wide[...] = chunks[c // 16, c % 16].astype(F32)
        for half in range(2):
            held[half, 36 * c : 36 * c + 36] = wide[36 * half : 36 * half + 36]
    for half in range(2):
        for kind in range(2):
            for b in range(6):
                start = 384 * b + 192 * kind
                outs[2 * half + kind][:, 128 * b : 128 * b + 128] = held[half, start : start + 192]


def spread_kernel(offs, where, s0, s1, s2, s3, out):
    total = None
    for k, slot in enumerate((s0, s1, s2, s3)):
        term = nn(spread_matrix(offs, where[0] ^ k), slot[...])
        total = term if total is None else total + term
    out[...] = total.astype(BF)


def swap(value, axis, k):
    count = lax.axis_size(axis)
    return lax.ppermute(value, axis, [(i, i ^ k) for i in range(count)])


def deal(value, axis):
    return lax.all_to_all(value, axis, 0, 0, tiled=True)


YZ_AXES = ("yh", "z")


def per_device(tokens, cotangent, w_query, w_key, w_value, w_out, offsets):
    where = jnp.stack([lax.axis_index(HEAD_AXES), lax.axis_index("x")]).astype(jnp.int32)

    def picked(source, first, rest, index):
        shape = ((192 * first + 64 * rest, WIDTH), BF)
        body = functools.partial(pick_kernel, first, rest)
        flops = 8 * shape[0][0] * 512 * 768
        return list(call(body, [shape] * 4, smem=2, flops=flops)(offsets, index, source))

    def to_heads(slots):
        return [slots[0]] + [swap(slots[k], HEAD_AXES, k) for k in (1, 2, 3)]

    tie = lax.optimization_barrier
    (joined,) = call(join_kernel, [((768, WIDTH), BF)])(w_query, w_key, w_value)
    token_rest = to_heads(picked(tokens, 0, 1, where))
    token_first, grad_rows = picked(tokens, 1, 0, where), picked(cotangent, 1, 1, where)
    token_rest[2], token_rest[3], token_first = tie((token_rest[2], token_rest[3], token_first))
    token_first, grad_rows = to_heads(token_first), to_heads(grad_rows)
    token_rest, token_first[0], grad_rows[0], joined = tie((token_rest, token_first[0], grad_rows[0], joined))

    half_chunks, full_chunks = ((16, 36, 128), BF), ((16, 72, 128), BF)
    halves = [((2304, 128), F32), ((4, 16, 36, 128), BF)]
    wide, half, short = ((3 * PER_HEAD, 128), BF), ((768, 128), BF), ((240, 128), BF)
    rest_shape, second_shape, third_shape = ((8, 240, 128), BF), ((8, 192, 128), BF), ((8, 48, 128), BF)
    whole_first, whole_rest = ((768, WIDTH), BF), ((240, WIDTH), BF)
    slot = ((SLOT, WIDTH), BF)

    x_rest, query_rest, rest = call(
        project_rest_kernel, [whole_rest, short, rest_shape], flops=2 * 240 * 768 * 256
    )(*token_rest, joined)
    rest, token_first[2] = tie((rest, token_first[2]))
    rest = deal(rest, "z")
    x_first, query_first, first = call(
        project_first_kernel, [whole_first, half, half], flops=2 * 768 * 768 * 256
    )(*token_first, joined)
    first_other = swap(first, "z", 1)
    third, x_first = tie((rest[:, 192:240], x_first))
    thirds = [swap(third, "x", j) for j in (1, 2, 3)]
    c_first, c_rest, grads = call(
        grad_rows_kernel, [whole_first, whole_rest, wide], flops=2 * 1008 * 768 * 128
    )(*grad_rows, w_out)

    attended, query_grad, first_back, first_send, second_back, *third_back = call(
        attention_kernel,
        [wide, wide, half, half, second_shape] + [third_shape] * 4,
        scratch=[((9, 512, 128), BF)],
        smem=2,
        flops=2 * 1008 * 512 * 128 * 7,
    )(offsets, where, query_first, query_rest, grads, first, first_other, rest, *thirds)

    third_got = [third_back[0]] + [swap(third_back[j], "x", j) for j in (1, 2, 3)]
    first_got = swap(first_send, "z", 1)
    early = call(early_kernel, [half_chunks] * 4, scratch=halves, smem=1, flops=4 * 1008 * 768 * 128)(
        where, attended, query_grad, c_first, c_rest, x_first, x_rest
    )
    mixed_slots = call(output_kernel, [slot] * 4, flops=2 * 1008 * 768 * 128)(attended, w_out)
    mixed_slots = to_heads(mixed_slots)
    early = [early[0]] + [swap(early[k], "x", k) for k in (1, 2, 3)]
    third_got, first_got, mixed_slots[0], early[0] = tie((third_got, first_got, mixed_slots[0], early[0]))
    (rest_back,) = call(third_sum_kernel, [rest_shape])(second_back, *third_got)
    rest_got = deal(rest_back, "z")
    rest_got, early = tie((rest_got, early))

    *late, changes = call(
        change_kernel,
        [half_chunks] * 4 + [((3 * PER_HEAD, 256), BF)],
        scratch=halves,
        smem=1,
        flops=2 * 1008 * 768 * 128,
    )(where, first_back, first_got, rest_got, query_grad, x_first, x_rest)
    late = [late[0]] + [swap(late[k], "x", k) for k in (1, 2, 3)]
    change_slots = call(input_kernel, [slot] * 4, flops=2 * 1008 * 768 * 256)(changes, joined)
    spread = call(spread_kernel, [((ROWS, WIDTH), BF)], smem=2, flops=2 * 1024 * 512 * 768)
    late, mixed_slots = tie((late, mixed_slots))
    (parts,) = call(x_sum_kernel, [full_chunks], scratch=[((72, 128), F32)])(*early, *late)
    (part,) = call(yz_sum_kernel, [full_chunks])(deal(parts, YZ_AXES))
    (mixed,) = spread(offsets, where, *mixed_slots)
    part, mixed, change_slots = tie((part, mixed, change_slots))
    block, change_slots = deal(part, YZ_AXES), to_heads(change_slots)
    blocks = [block] + [swap(block, "x", k) for k in (1, 2, 3)]
    (grad_tokens,) = spread(offsets, where, *change_slots)
    grad_query, grad_out, grad_key, grad_value = call(
        place_kernel,
        [((192, WIDTH), F32)] * 4,
        scratch=[((4, 16, 72, 128), BF), ((72, 128), F32), ((2, 2304, 128), F32)],
        smem=1,
    )(where, *blocks)
    return mixed, grad_tokens, grad_query, grad_key, grad_value, grad_out


def solution(mesh):
    fine = jax.sharding.Mesh(mesh.devices.reshape(2, 4, 8, 2, 2), ("yh", "x", "z", "yl", "core"))
    rows = P(("yh", "x", "z", "yl", "core"), None)
    cut = P(HEAD_AXES, None)
    return jax.shard_map(
        per_device,
        mesh=fine,
        in_specs=(rows, rows, cut, cut, cut, cut, P()),
        out_specs=(rows, rows, cut, cut, cut, cut),
        check_vma=False,
    )
```

```python
import functools

import jax
import jax.numpy as jnp
from jax import lax
from jax.experimental import pallas as pl
from jax.experimental.pallas import tpu as pltpu
from jax.sharding import PartitionSpec as P

BF = jnp.bfloat16
F32 = jnp.float32
WIDTH = 768
ROWS = 512
SLOT = 256
PER_HEAD = 336
SPANS = ((0, 256), (256, 320), (320, 336))
SCALE = 0.125
HEAD_AXES = ("yl", "core")


def nn(a, b):
    return jnp.dot(a, b, preferred_element_type=F32)


def nt(a, b):
    return lax.dot_general(a, b, (((1,), (1,)), ((), ())), preferred_element_type=F32)


def tn(a, b):
    return lax.dot_general(a, b, (((0,), (0,)), ((), ())), preferred_element_type=F32)


def iota(shape, dim):
    return lax.broadcasted_iota(jnp.int32, shape, dim)


def ones_where(mask):
    return jnp.where(mask, 1.0, 0.0).astype(BF)


def pick_first(offs, group):
    row, col = iota((64, ROWS), 0), iota((64, ROWS), 1)
    return jnp.concatenate([ones_where(8 * row + offs[0, 3 * group + a] == col) for a in range(3)], 0)


def pick_rest(offs, group):
    row, col = iota((16, ROWS), 0), iota((16, ROWS), 1)
    parts = [ones_where(32 * row + offs[1, 3 * group + a] == col) for a in range(3)]
    third = [offs[2, 3 * group + a] for a in range(3)]
    off = jnp.where(row < 4, third[0], jnp.where(row < 8, third[1], jnp.where(row < 12, third[2], 4 * ROWS)))
    parts.append(ones_where(128 * (row & 3) + off == col))
    return jnp.concatenate(parts, 0)


def spread_matrix(offs, group):
    lane = iota((1, SLOT), 1)
    o = [[offs[level, 3 * group + a] for a in range(3)] for level in range(3)]
    first = 8 * (lane & 63) + jnp.where(lane < 64, o[0][0], jnp.where(lane < 128, o[0][1], o[0][2]))
    second = 32 * (lane & 15) + jnp.where(lane < 208, o[1][0], jnp.where(lane < 224, o[1][1], o[1][2]))
    third = 128 * (lane & 3) + jnp.where(
        lane < 244, o[2][0], jnp.where(lane < 248, o[2][1], jnp.where(lane < 252, o[2][2], 4 * ROWS))
    )
    pos = jnp.where(lane < 192, first, jnp.where(lane < 240, second, third))
    return ones_where(iota((ROWS, SLOT), 0) == pos)


def third_order(dim):
    new, old = iota((64, 64), dim), iota((64, 64), 1 - dim)
    source = 16 * ((new >> 2) & 3) + 4 * (new >> 4) + (new & 3)
    return ones_where((source == old) & (new < 48))


def call(body, outs, scratch=(), smem=0, flops=0, nbytes=4 << 20):
    def run(*args):
        vmem = pl.BlockSpec(memory_space=pltpu.VMEM)
        specs = [pl.BlockSpec(memory_space=pltpu.SMEM)] * smem + [vmem] * (len(args) - smem)
        return pl.pallas_call(
            body,
            out_shape=tuple(jax.ShapeDtypeStruct(shape, kind) for shape, kind in outs),
            in_specs=specs,
            out_specs=tuple(vmem for _ in outs),
            scratch_shapes=[pltpu.VMEM(shape, kind) for shape, kind in scratch],
            compiler_params=pltpu.CompilerParams(vmem_limit_bytes=40 << 20),
            cost_estimate=pl.CostEstimate(flops=flops, bytes_accessed=nbytes, transcendentals=0),
        )(*args)

    return run


def pick_kernel(first, rest, offs, where, source, *outs):
    for k in (2, 3, 1, 0):
        group = where[0] ^ k
        parts = ([pick_first(offs, group)] if first else []) + ([pick_rest(offs, group)] if rest else [])
        outs[k][...] = nn(jnp.concatenate(parts, 0), source[...]).astype(BF)


def regroup_rest(rests, whole):
    third = jnp.concatenate([rest[48:64] for rest in rests], 0)
    third = nn(third_order(0), third).astype(BF)
    for a in range(3):
        for k in range(4):
            whole[80 * a + 16 * k : 80 * a + 16 * k + 16] = rests[k][16 * a : 16 * a + 16]
        whole[80 * a + 64 : 80 * a + 80] = third[16 * a : 16 * a + 16]


def regroup_first(firsts, whole):
    for a in range(3):
        for k in range(4):
            whole[256 * a + 64 * k : 256 * a + 64 * k + 64] = firsts[k][64 * a : 64 * a + 64]


def ungroup(parts, slots):
    third = jnp.concatenate([part[320:336] for part in parts] + [jnp.zeros((16, WIDTH), BF)], 0)
    third = nn(third_order(1), third).astype(BF)
    for k in range(4):
        for a in range(3):
            slots[k][64 * a : 64 * a + 64] = parts[a][64 * k : 64 * k + 64]
            slots[k][192 + 16 * a : 208 + 16 * a] = parts[a][256 + 16 * k : 272 + 16 * k]
        slots[k][240:256] = third[16 * k : 16 * k + 16]


def join_kernel(w_query, w_key, w_value, joined):
    for a in range(3):
        own = slice(64 * a, 64 * a + 64)
        joined[256 * a : 256 * a + 64] = w_key[own]
        joined[256 * a + 64 : 256 * a + 128] = w_value[own]
        joined[256 * a + 128 : 256 * a + 192] = w_query[own]
        joined[256 * a + 192 : 256 * a + 256] = jnp.zeros((64, WIDTH), BF)


def pad_out(w_out, a):
    return jnp.concatenate([jnp.zeros((64, WIDTH), BF), w_out[64 * a : 64 * a + 64]], 0)


def project_rest_kernel(x0, x1, x2, x3, joined, whole, query, rest):
    regroup_rest((x0, x1, x2, x3), whole)
    for a in range(3):
        made = nt(whole[80 * a : 80 * a + 80], joined[256 * a : 256 * a + 256]).astype(BF)
        query[80 * a : 80 * a + 80] = made[:, 128:256]
        for k in range(8):
            rest[k, 64 * a : 64 * a + 64] = made[0:64, 0:128]
            rest[k, 192 + 16 * a : 208 + 16 * a] = made[64:80, 0:128]


def project_first_kernel(x0, x1, x2, x3, joined, whole, query, first):
    regroup_first((x0, x1, x2, x3), whole)
    for a in range(3):
        own = slice(256 * a, 256 * a + 256)
        made = nt(whole[own], joined[own]).astype(BF)
        query[own] = made[:, 128:256]
        first[own] = made[:, 0:128]


def rows_of(first, rest, a):
    return jnp.concatenate([first[256 * a : 256 * a + 256], rest[80 * a : 80 * a + 80]], 0)


def grad_rows_kernel(c0, c1, c2, c3, w_out, whole_first, whole_rest, grads):
    slots = (c0, c1, c2, c3)
    regroup_first(slots, whole_first)
    regroup_rest([slot.at[192:256] for slot in slots], whole_rest)
    for a in range(3):
        base = PER_HEAD * a
        grads[base : base + PER_HEAD] = nt(rows_of(whole_first, whole_rest, a), pad_out(w_out, a)).astype(BF)


def attention_kernel(offs, where, query_first, query_rest, grads, first_own, first_other, rest, *refs):
    thirds = refs[:3]
    attended, query_grad, first_back, first_send, second_back = refs[3:8]
    third_back, keys = refs[8:12], refs[12]
    for a in range(3):
        keys[a, 0:256] = first_own[256 * a : 256 * a + 256]
        keys[a, 256:512] = first_other[256 * a : 256 * a + 256]
        for k in range(8):
            keys[3 + a, 64 * k : 64 * k + 64] = rest[k, 64 * a : 64 * a + 64]
            keys[6 + a, 16 * k : 16 * k + 16] = rest[k, 192 + 16 * a : 208 + 16 * a]
            for j in range(3):
                keys[6 + a, 128 * (j + 1) + 16 * k : 128 * (j + 1) + 16 * k + 16] = thirds[j][
                    k, 16 * a : 16 * a + 16
                ]

    def position(index, a):
        o = [offs[level, 3 * where[0] + a] for level in range(3)]
        return jnp.where(
            index < 256,
            8 * index + o[0],
            jnp.where(index < 320, 32 * (index - 256) + o[1], 128 * (index - 320) + o[2]),
        )

    for a in range(3):
        base = PER_HEAD * a
        q, g = rows_of(query_first, query_rest, a), grads[base : base + PER_HEAD]
        same = ones_where(position(iota((PER_HEAD, 1), 0), a) == position(iota((1, PER_HEAD), 1), a))

        def over_levels(column):
            high = column.astype(BF).astype(F32)
            middle = (column - high).astype(BF).astype(F32)
            lane = iota((PER_HEAD, 128), 1)
            parts = jnp.where(
                lane == 0, high, jnp.where(lane == 1, middle, jnp.where(lane == 2, column - high - middle, 0.0))
            )
            return jnp.sum(nn(same, parts.astype(BF)), 1, keepdims=True)

        expo = [
            jnp.exp(nt(q[low:high], keys[3 * level + a]) * SCALE) for level, (low, high) in enumerate(SPANS)
        ]
        total = over_levels(jnp.concatenate([jnp.sum(e, 1, keepdims=True) for e in expo], 0))
        inverse = 1.0 / total
        weights = [e * inverse[low:high] for e, (low, high) in zip(expo, SPANS)]
        rounded = [w.astype(BF) for w in weights]
        out = jnp.concatenate([nn(rounded[level], keys[3 * level + a]) for level in range(3)], 0)
        attended[base : base + PER_HEAD] = out.astype(BF)
        delta = over_levels(jnp.sum(g.astype(F32) * out, 1, keepdims=True))
        for level, (low, high) in enumerate(SPANS):
            block = keys[3 * level + a]
            back = nt(g[low:high], block)
            score = (weights[level] * (back - delta[low:high]) * SCALE).astype(BF)
            query_grad[base + low : base + high] = nn(score, block).astype(BF)
            pair = (tn(score, q[low:high]) + tn(rounded[level], g[low:high])).astype(BF)
            if level == 0:
                first_back[256 * a : 256 * a + 256] = pair[0:256]
                first_send[256 * a : 256 * a + 256] = pair[256:512]
            elif level == 1:
                for k in range(8):
                    second_back[k, 64 * a : 64 * a + 64] = pair[64 * k : 64 * k + 64]
            else:
                for j in range(4):
                    for k in range(8):
                        third_back[j][k, 16 * a : 16 * a + 16] = pair[128 * j + 16 * k : 128 * j + 16 * k + 16]


def put_chunks(place, held, chunks, sends):
    for c in range(64):
        chunks[c // 16, c % 16] = held[36 * c : 36 * c + 36].astype(BF)
    for k in range(4):
        sends[k][...] = chunks[place[1] ^ k]


def put_grad(held, kind, a, value):
    for b in range(6):
        start = 384 * b + 192 * kind + 64 * a
        held[start : start + 64] = value[:, 128 * b : 128 * b + 128]


def early_kernel(place, attended, query_grad, c_first, c_rest, x_first, x_rest, *refs):
    sends, held, chunks = refs[:4], refs[4], refs[5]
    for a in range(3):
        own = slice(PER_HEAD * a, PER_HEAD * a + PER_HEAD)
        put_grad(held, 0, a, tn(query_grad[own], rows_of(x_first, x_rest, a))[0:64])
        put_grad(held, 1, a, tn(attended[own], rows_of(c_first, c_rest, a))[64:128])
    put_chunks(place, held, chunks, sends)


def output_kernel(attended, w_out, s0, s1, s2, s3):
    parts = []
    for a in range(3):
        own = slice(PER_HEAD * a, PER_HEAD * a + PER_HEAD)
        parts.append(nn(attended[own], pad_out(w_out, a)).astype(BF))
    ungroup(parts, (s0, s1, s2, s3))


def total_of(parts, count):
    return functools.reduce(lambda x, y: x + y, [parts[k].astype(F32) for k in range(count)])


def third_sum_kernel(second, t0, t1, t2, t3, sends):
    for k in range(8):
        sends[k, 0:192] = second[k]
        sends[k, 192:240] = total_of([t[k] for t in (t0, t1, t2, t3)], 4).astype(BF)


def change_kernel(place, first_own, first_other, rests, query_grad, x_first, x_rest, *refs):
    sends, changes, held, chunks = refs[:4], refs[4], refs[5], refs[6]
    first = first_own[...].astype(F32) + first_other[...].astype(F32)
    rest = total_of(rests, 8)
    for a in range(3):
        own = slice(PER_HEAD * a, PER_HEAD * a + PER_HEAD)
        pair = jnp.concatenate(
            [first[256 * a : 256 * a + 256], rest[64 * a : 64 * a + 64], rest[192 + 16 * a : 208 + 16 * a]], 0
        ).astype(BF)
        made = tn(pair, rows_of(x_first, x_rest, a))
        put_grad(held, 0, a, made[0:64])
        put_grad(held, 1, a, made[64:128])
        changes[own] = jnp.concatenate([pair, query_grad[own]], 1)
    put_chunks(place, held, chunks, sends)


def input_kernel(changes, joined, s0, s1, s2, s3):
    parts = []
    for a in range(3):
        own = slice(PER_HEAD * a, PER_HEAD * a + PER_HEAD)
        parts.append(nn(changes[own], joined[256 * a : 256 * a + 256]).astype(BF))
    ungroup(parts, (s0, s1, s2, s3))


def x_sum_kernel(*refs):
    out, held = refs[8], refs[9]
    for y in range(16):
        for half in range(2):
            held[36 * half : 36 * half + 36] = total_of([part[y] for part in refs[4 * half : 4 * half + 4]], 4)
        out[y] = held[...].astype(BF)


def yz_sum_kernel(got, sends):
    total = total_of(got, 16).astype(BF)
    for y in range(16):
        sends[y] = total


def place_kernel(place, b0, b1, b2, b3, *refs):
    outs, chunks, wide, held = refs[:4], refs[4], refs[5], refs[6]
    for k, block in enumerate((b0, b1, b2, b3)):
        chunks[place[1] ^ k] = block[...]
    for c in range(64):
        wide[...] = chunks[c // 16, c % 16].astype(F32)
        for half in range(2):
            held[half, 36 * c : 36 * c + 36] = wide[36 * half : 36 * half + 36]
    for half in range(2):
        for kind in range(2):
            for b in range(6):
                start = 384 * b + 192 * kind
                outs[2 * half + kind][:, 128 * b : 128 * b + 128] = held[half, start : start + 192]


def spread_kernel(offs, where, s0, s1, s2, s3, out):
    total = None
    for k, slot in enumerate((s0, s1, s2, s3)):
        term = nn(spread_matrix(offs, where[0] ^ k), slot[...])
        total = term if total is None else total + term
    out[...] = total.astype(BF)


def swap(value, axis, k):
    count = lax.axis_size(axis)
    return lax.ppermute(value, axis, [(i, i ^ k) for i in range(count)])


def deal(value, axis):
    return lax.all_to_all(value, axis, 0, 0, tiled=True)


YZ_AXES = ("yh", "z")


def per_device(tokens, cotangent, w_query, w_key, w_value, w_out, offsets):
    where = jnp.stack([lax.axis_index(HEAD_AXES), lax.axis_index("x")]).astype(jnp.int32)

    def picked(source, first, rest, index):
        shape = ((192 * first + 64 * rest, WIDTH), BF)
        body = functools.partial(pick_kernel, first, rest)
        flops = 8 * shape[0][0] * 512 * 768
        return list(call(body, [shape] * 4, smem=2, flops=flops)(offsets, index, source))

    def to_heads(slots):
        return [slots[0]] + [swap(slots[k], HEAD_AXES, k) for k in (1, 2, 3)]

    tie = lax.optimization_barrier
    (joined,) = call(join_kernel, [((768, WIDTH), BF)])(w_query, w_key, w_value)
    token_rest = to_heads(picked(tokens, 0, 1, where))
    token_first, grad_rows = picked(tokens, 1, 0, where), picked(cotangent, 1, 1, where)
    token_rest[2], token_rest[3], token_first = tie((token_rest[2], token_rest[3], token_first))
    token_first, grad_rows = to_heads(token_first), to_heads(grad_rows)
    token_rest, token_first[0], grad_rows[0], joined = tie((token_rest, token_first[0], grad_rows[0], joined))

    half_chunks, full_chunks = ((16, 36, 128), BF), ((16, 72, 128), BF)
    halves = [((2304, 128), F32), ((4, 16, 36, 128), BF)]
    wide, half, short = ((3 * PER_HEAD, 128), BF), ((768, 128), BF), ((240, 128), BF)
    rest_shape, second_shape, third_shape = ((8, 240, 128), BF), ((8, 192, 128), BF), ((8, 48, 128), BF)
    whole_first, whole_rest = ((768, WIDTH), BF), ((240, WIDTH), BF)
    slot = ((SLOT, WIDTH), BF)

    x_rest, query_rest, rest = call(
        project_rest_kernel, [whole_rest, short, rest_shape], flops=2 * 240 * 768 * 256
    )(*token_rest, joined)
    rest, token_first[2] = tie((rest, token_first[2]))
    rest = deal(rest, "z")
    x_first, query_first, first = call(
        project_first_kernel, [whole_first, half, half], flops=2 * 768 * 768 * 256
    )(*token_first, joined)
    first_other = swap(first, "z", 1)
    third, x_first = tie((rest[:, 192:240], x_first))
    thirds = [swap(third, "x", j) for j in (1, 2, 3)]
    c_first, c_rest, grads = call(
        grad_rows_kernel, [whole_first, whole_rest, wide], flops=2 * 1008 * 768 * 128
    )(*grad_rows, w_out)

    attended, query_grad, first_back, first_send, second_back, *third_back = call(
        attention_kernel,
        [wide, wide, half, half, second_shape] + [third_shape] * 4,
        scratch=[((9, 512, 128), BF)],
        smem=2,
        flops=2 * 1008 * 512 * 128 * 7,
    )(offsets, where, query_first, query_rest, grads, first, first_other, rest, *thirds)

    third_got = [third_back[0]] + [swap(third_back[j], "x", j) for j in (1, 2, 3)]
    first_got = swap(first_send, "z", 1)
    early = call(early_kernel, [half_chunks] * 4, scratch=halves, smem=1, flops=4 * 1008 * 768 * 128)(
        where, attended, query_grad, c_first, c_rest, x_first, x_rest
    )
    mixed_slots = call(output_kernel, [slot] * 4, flops=2 * 1008 * 768 * 128)(attended, w_out)
    mixed_slots = to_heads(mixed_slots)
    early = [early[0]] + [swap(early[k], "x", k) for k in (1, 2, 3)]
    third_got, first_got, early[0] = tie((third_got, first_got, early[0]))
    (rest_back,) = call(third_sum_kernel, [rest_shape])(second_back, *third_got)
    rest_got = deal(rest_back, "z")
    rest_got, early = tie((rest_got, early))

    *late, changes = call(
        change_kernel,
        [half_chunks] * 4 + [((3 * PER_HEAD, 256), BF)],
        scratch=halves,
        smem=1,
        flops=2 * 1008 * 768 * 128,
    )(where, first_back, first_got, rest_got, query_grad, x_first, x_rest)
    late = [late[0]] + [swap(late[k], "x", k) for k in (1, 2, 3)]
    change_slots = call(input_kernel, [slot] * 4, flops=2 * 1008 * 768 * 256)(changes, joined)
    spread = call(spread_kernel, [((ROWS, WIDTH), BF)], smem=2, flops=2 * 1024 * 512 * 768)
    late, mixed_slots = tie((late, mixed_slots))
    (parts,) = call(x_sum_kernel, [full_chunks], scratch=[((72, 128), F32)])(*early, *late)
    (part,) = call(yz_sum_kernel, [full_chunks])(deal(parts, YZ_AXES))
    (mixed,) = spread(offsets, where, *mixed_slots)
    part, mixed, change_slots = tie((part, mixed, change_slots))
    block, change_slots = deal(part, YZ_AXES), to_heads(change_slots)
    blocks = [block] + [swap(block, "x", k) for k in (1, 2, 3)]
    (grad_tokens,) = spread(offsets, where, *change_slots)
    grad_query, grad_out, grad_key, grad_value = call(
        place_kernel,
        [((192, WIDTH), F32)] * 4,
        scratch=[((4, 16, 72, 128), BF), ((72, 128), F32), ((2, 2304, 128), F32)],
        smem=1,
    )(where, *blocks)
    return mixed, grad_tokens, grad_query, grad_key, grad_value, grad_out


def solution(mesh):
    fine = jax.sharding.Mesh(mesh.devices.reshape(2, 4, 8, 2, 2), ("yh", "x", "z", "yl", "core"))
    rows = P(("yh", "x", "z", "yl", "core"), None)
    cut = P(HEAD_AXES, None)
    return jax.shard_map(
        per_device,
        mesh=fine,
        in_specs=(rows, rows, cut, cut, cut, cut, P()),
        out_specs=(rows, rows, cut, cut, cut, cut),
        check_vma=False,
    )
```

```python
import functools

import jax
import jax.numpy as jnp
from jax import lax
from jax.experimental import pallas as pl
from jax.experimental.pallas import tpu as pltpu
from jax.sharding import PartitionSpec as P

BF = jnp.bfloat16
F32 = jnp.float32
WIDTH = 768
ROWS = 512
SLOT = 256
PER_HEAD = 336
SPANS = ((0, 256), (256, 320), (320, 336))
SCALE = 0.125
HEAD_AXES = ("yl", "core")


def nn(a, b):
    return jnp.dot(a, b, preferred_element_type=F32)


def nt(a, b):
    return lax.dot_general(a, b, (((1,), (1,)), ((), ())), preferred_element_type=F32)


def tn(a, b):
    return lax.dot_general(a, b, (((0,), (0,)), ((), ())), preferred_element_type=F32)


def iota(shape, dim):
    return lax.broadcasted_iota(jnp.int32, shape, dim)


def ones_where(mask):
    return jnp.where(mask, 1.0, 0.0).astype(BF)


def pick_first(offs, group):
    row, col = iota((64, ROWS), 0), iota((64, ROWS), 1)
    return jnp.concatenate([ones_where(8 * row + offs[0, 3 * group + a] == col) for a in range(3)], 0)


def pick_rest(offs, group):
    row, col = iota((16, ROWS), 0), iota((16, ROWS), 1)
    parts = [ones_where(32 * row + offs[1, 3 * group + a] == col) for a in range(3)]
    third = [offs[2, 3 * group + a] for a in range(3)]
    off = jnp.where(row < 4, third[0], jnp.where(row < 8, third[1], jnp.where(row < 12, third[2], 4 * ROWS)))
    parts.append(ones_where(128 * (row & 3) + off == col))
    return jnp.concatenate(parts, 0)


def spread_matrix(offs, group):
    lane = iota((1, SLOT), 1)
    o = [[offs[level, 3 * group + a] for a in range(3)] for level in range(3)]
    first = 8 * (lane & 63) + jnp.where(lane < 64, o[0][0], jnp.where(lane < 128, o[0][1], o[0][2]))
    second = 32 * (lane & 15) + jnp.where(lane < 208, o[1][0], jnp.where(lane < 224, o[1][1], o[1][2]))
    third = 128 * (lane & 3) + jnp.where(
        lane < 244, o[2][0], jnp.where(lane < 248, o[2][1], jnp.where(lane < 252, o[2][2], 4 * ROWS))
    )
    pos = jnp.where(lane < 192, first, jnp.where(lane < 240, second, third))
    return ones_where(iota((ROWS, SLOT), 0) == pos)


def third_order(dim):
    new, old = iota((64, 64), dim), iota((64, 64), 1 - dim)
    source = 16 * ((new >> 2) & 3) + 4 * (new >> 4) + (new & 3)
    return ones_where((source == old) & (new < 48))


def call(body, outs, scratch=(), smem=0, flops=0, nbytes=4 << 20):
    def run(*args):
        vmem = pl.BlockSpec(memory_space=pltpu.VMEM)
        specs = [pl.BlockSpec(memory_space=pltpu.SMEM)] * smem + [vmem] * (len(args) - smem)
        return pl.pallas_call(
            body,
            out_shape=tuple(jax.ShapeDtypeStruct(shape, kind) for shape, kind in outs),
            in_specs=specs,
            out_specs=tuple(vmem for _ in outs),
            scratch_shapes=[pltpu.VMEM(shape, kind) for shape, kind in scratch],
            compiler_params=pltpu.CompilerParams(vmem_limit_bytes=40 << 20),
            cost_estimate=pl.CostEstimate(flops=flops, bytes_accessed=nbytes, transcendentals=0),
        )(*args)

    return run


def pick_kernel(first, rest, offs, where, source, *outs):
    for k in (2, 3, 1, 0):
        group = where[0] ^ k
        parts = ([pick_first(offs, group)] if first else []) + ([pick_rest(offs, group)] if rest else [])
        outs[k][...] = nn(jnp.concatenate(parts, 0), source[...]).astype(BF)


def regroup_rest(rests, whole):
    third = jnp.concatenate([rest[48:64] for rest in rests], 0)
    third = nn(third_order(0), third).astype(BF)
    for a in range(3):
        for k in range(4):
            whole[80 * a + 16 * k : 80 * a + 16 * k + 16] = rests[k][16 * a : 16 * a + 16]
        whole[80 * a + 64 : 80 * a + 80] = third[16 * a : 16 * a + 16]


def regroup_first(firsts, whole):
    for a in range(3):
        for k in range(4):
            whole[256 * a + 64 * k : 256 * a + 64 * k + 64] = firsts[k][64 * a : 64 * a + 64]


def ungroup(parts, slots):
    third = jnp.concatenate([part[320:336] for part in parts] + [jnp.zeros((16, WIDTH), BF)], 0)
    third = nn(third_order(1), third).astype(BF)
    for k in range(4):
        for a in range(3):
            slots[k][64 * a : 64 * a + 64] = parts[a][64 * k : 64 * k + 64]
            slots[k][192 + 16 * a : 208 + 16 * a] = parts[a][256 + 16 * k : 272 + 16 * k]
        slots[k][240:256] = third[16 * k : 16 * k + 16]


def join_kernel(w_query, w_key, w_value, joined):
    for a in range(3):
        own = slice(64 * a, 64 * a + 64)
        joined[256 * a : 256 * a + 64] = w_key[own]
        joined[256 * a + 64 : 256 * a + 128] = w_value[own]
        joined[256 * a + 128 : 256 * a + 192] = w_query[own]
        joined[256 * a + 192 : 256 * a + 256] = jnp.zeros((64, WIDTH), BF)


def pad_out(w_out, a):
    return jnp.concatenate([jnp.zeros((64, WIDTH), BF), w_out[64 * a : 64 * a + 64]], 0)


def project_rest_kernel(x0, x1, x2, x3, joined, whole, query, rest):
    regroup_rest((x0, x1, x2, x3), whole)
    for a in range(3):
        made = nt(whole[80 * a : 80 * a + 80], joined[256 * a : 256 * a + 256]).astype(BF)
        query[80 * a : 80 * a + 80] = made[:, 128:256]
        for k in range(8):
            rest[k, 64 * a : 64 * a + 64] = made[0:64, 0:128]
            rest[k, 192 + 16 * a : 208 + 16 * a] = made[64:80, 0:128]


def project_first_kernel(x0, x1, x2, x3, joined, whole, query, first):
    regroup_first((x0, x1, x2, x3), whole)
    for a in range(3):
        own = slice(256 * a, 256 * a + 256)
        made = nt(whole[own], joined[own]).astype(BF)
        query[own] = made[:, 128:256]
        first[own] = made[:, 0:128]


def rows_of(first, rest, a):
    return jnp.concatenate([first[256 * a : 256 * a + 256], rest[80 * a : 80 * a + 80]], 0)


def grad_rows_kernel(c0, c1, c2, c3, w_out, whole_first, whole_rest, grads):
    slots = (c0, c1, c2, c3)
    regroup_first(slots, whole_first)
    regroup_rest([slot.at[192:256] for slot in slots], whole_rest)
    for a in range(3):
        base = PER_HEAD * a
        grads[base : base + PER_HEAD] = nt(rows_of(whole_first, whole_rest, a), pad_out(w_out, a)).astype(BF)


def attention_kernel(offs, where, query_first, query_rest, grads, first_own, first_other, rest, *refs):
    thirds = refs[:3]
    attended, query_grad, first_back, first_send, second_back = refs[3:8]
    third_back, keys = refs[8:12], refs[12]
    for a in range(3):
        keys[a, 0:256] = first_own[256 * a : 256 * a + 256]
        keys[a, 256:512] = first_other[256 * a : 256 * a + 256]
        for k in range(8):
            keys[3 + a, 64 * k : 64 * k + 64] = rest[k, 64 * a : 64 * a + 64]
            keys[6 + a, 16 * k : 16 * k + 16] = rest[k, 192 + 16 * a : 208 + 16 * a]
            for j in range(3):
                keys[6 + a, 128 * (j + 1) + 16 * k : 128 * (j + 1) + 16 * k + 16] = thirds[j][
                    k, 16 * a : 16 * a + 16
                ]

    def position(index, a):
        o = [offs[level, 3 * where[0] + a] for level in range(3)]
        return jnp.where(
            index < 256,
            8 * index + o[0],
            jnp.where(index < 320, 32 * (index - 256) + o[1], 128 * (index - 320) + o[2]),
        )

    for a in range(3):
        base = PER_HEAD * a
        q, g = rows_of(query_first, query_rest, a), grads[base : base + PER_HEAD]
        same = ones_where(position(iota((PER_HEAD, 1), 0), a) == position(iota((1, PER_HEAD), 1), a))

        def over_levels(column):
            high = column.astype(BF).astype(F32)
            middle = (column - high).astype(BF).astype(F32)
            lane = iota((PER_HEAD, 128), 1)
            parts = jnp.where(
                lane == 0, high, jnp.where(lane == 1, middle, jnp.where(lane == 2, column - high - middle, 0.0))
            )
            return jnp.sum(nn(same, parts.astype(BF)), 1, keepdims=True)

        expo = [
            jnp.exp(nt(q[low:high], keys[3 * level + a]) * SCALE) for level, (low, high) in enumerate(SPANS)
        ]
        total = over_levels(jnp.concatenate([jnp.sum(e, 1, keepdims=True) for e in expo], 0))
        inverse = 1.0 / total
        weights = [e * inverse[low:high] for e, (low, high) in zip(expo, SPANS)]
        rounded = [w.astype(BF) for w in weights]
        out = jnp.concatenate([nn(rounded[level], keys[3 * level + a]) for level in range(3)], 0)
        attended[base : base + PER_HEAD] = out.astype(BF)
        delta = over_levels(jnp.sum(g.astype(F32) * out, 1, keepdims=True))
        for level, (low, high) in enumerate(SPANS):
            block = keys[3 * level + a]
            back = nt(g[low:high], block)
            score = (weights[level] * (back - delta[low:high]) * SCALE).astype(BF)
            query_grad[base + low : base + high] = nn(score, block).astype(BF)
            pair = (tn(score, q[low:high]) + tn(rounded[level], g[low:high])).astype(BF)
            if level == 0:
                first_back[256 * a : 256 * a + 256] = pair[0:256]
                first_send[256 * a : 256 * a + 256] = pair[256:512]
            elif level == 1:
                for k in range(8):
                    second_back[k, 64 * a : 64 * a + 64] = pair[64 * k : 64 * k + 64]
            else:
                for j in range(4):
                    for k in range(8):
                        third_back[j][k, 16 * a : 16 * a + 16] = pair[128 * j + 16 * k : 128 * j + 16 * k + 16]


def put_chunks(place, held, chunks, sends):
    for c in range(4):
        chunks[c] = held[576 * c : 576 * c + 576].astype(BF)
    for k in range(4):
        sends[k][...] = chunks[place[1] ^ k]


def put_grad(held, kind, a, value):
    for b in range(6):
        start = 384 * b + 192 * kind + 64 * a
        held[start : start + 64] = value[:, 128 * b : 128 * b + 128]


def early_kernel(place, attended, query_grad, c_first, c_rest, x_first, x_rest, *refs):
    sends, held, chunks = refs[:4], refs[4], refs[5]
    for a in range(3):
        own = slice(PER_HEAD * a, PER_HEAD * a + PER_HEAD)
        put_grad(held, 0, a, tn(query_grad[own], rows_of(x_first, x_rest, a))[0:64])
        put_grad(held, 1, a, tn(attended[own], rows_of(c_first, c_rest, a))[64:128])
    put_chunks(place, held, chunks, sends)


def output_kernel(attended, w_out, s0, s1, s2, s3):
    parts = []
    for a in range(3):
        own = slice(PER_HEAD * a, PER_HEAD * a + PER_HEAD)
        parts.append(nn(attended[own], pad_out(w_out, a)).astype(BF))
    ungroup(parts, (s0, s1, s2, s3))


def total_of(parts, count):
    return functools.reduce(lambda x, y: x + y, [parts[k].astype(F32) for k in range(count)])


def third_sum_kernel(second, t0, t1, t2, t3, sends):
    for k in range(8):
        sends[k, 0:192] = second[k]
        sends[k, 192:240] = total_of([t[k] for t in (t0, t1, t2, t3)], 4).astype(BF)


def change_kernel(place, first_own, first_other, rests, query_grad, x_first, x_rest, *refs):
    sends, changes, held, chunks = refs[:4], refs[4], refs[5], refs[6]
    first = first_own[...].astype(F32) + first_other[...].astype(F32)
    rest = total_of(rests, 8)
    for a in range(3):
        own = slice(PER_HEAD * a, PER_HEAD * a + PER_HEAD)
        pair = jnp.concatenate(
            [first[256 * a : 256 * a + 256], rest[64 * a : 64 * a + 64], rest[192 + 16 * a : 208 + 16 * a]], 0
        ).astype(BF)
        made = tn(pair, rows_of(x_first, x_rest, a))
        put_grad(held, 0, a, made[0:64])
        put_grad(held, 1, a, made[64:128])
        changes[own] = jnp.concatenate([pair, query_grad[own]], 1)
    put_chunks(place, held, chunks, sends)


def input_kernel(changes, joined, s0, s1, s2, s3):
    parts = []
    for a in range(3):
        own = slice(PER_HEAD * a, PER_HEAD * a + PER_HEAD)
        parts.append(nn(changes[own], joined[256 * a : 256 * a + 256]).astype(BF))
    ungroup(parts, (s0, s1, s2, s3))


def x_sum_kernel(*refs):
    out, total, held = refs[8:]
    for half in range(2):
        total[half] = total_of([part[...] for part in refs[4 * half : 4 * half + 4]], 4)
    for y in range(16):
        for half in range(2):
            held[36 * half : 36 * half + 36] = total[half, 36 * y : 36 * y + 36]
        out[y] = held[...].astype(BF)


def yz_sum_kernel(got, sends):
    total = total_of(got, 16).astype(BF)
    for y in range(16):
        sends[y] = total


def place_kernel(place, b0, b1, b2, b3, *refs):
    outs, chunks, wide, held = refs[:4], refs[4], refs[5], refs[6]
    for k, block in enumerate((b0, b1, b2, b3)):
        chunks[place[1] ^ k] = block[...]
    for c in range(64):
        wide[...] = chunks[c // 16, c % 16].astype(F32)
        for half in range(2):
            held[half, 36 * c : 36 * c + 36] = wide[36 * half : 36 * half + 36]
    for half in range(2):
        for kind in range(2):
            for b in range(6):
                start = 384 * b + 192 * kind
                outs[2 * half + kind][:, 128 * b : 128 * b + 128] = held[half, start : start + 192]


def spread_kernel(offs, where, s0, s1, s2, s3, out):
    total = None
    for k, slot in enumerate((s0, s1, s2, s3)):
        term = nn(spread_matrix(offs, where[0] ^ k), slot[...])
        total = term if total is None else total + term
    out[...] = total.astype(BF)


def swap(value, axis, k):
    count = lax.axis_size(axis)
    return lax.ppermute(value, axis, [(i, i ^ k) for i in range(count)])


def deal(value, axis):
    return lax.all_to_all(value, axis, 0, 0, tiled=True)


YZ_AXES = ("yh", "z")


def per_device(tokens, cotangent, w_query, w_key, w_value, w_out, offsets):
    where = jnp.stack([lax.axis_index(HEAD_AXES), lax.axis_index("x")]).astype(jnp.int32)

    def picked(source, first, rest, index):
        shape = ((192 * first + 64 * rest, WIDTH), BF)
        body = functools.partial(pick_kernel, first, rest)
        flops = 8 * shape[0][0] * 512 * 768
        return list(call(body, [shape] * 4, smem=2, flops=flops)(offsets, index, source))

    def to_heads(slots):
        return [slots[0]] + [swap(slots[k], HEAD_AXES, k) for k in (1, 2, 3)]

    tie = lax.optimization_barrier
    (joined,) = call(join_kernel, [((768, WIDTH), BF)])(w_query, w_key, w_value)
    token_rest = to_heads(picked(tokens, 0, 1, where))
    token_first, grad_rows = picked(tokens, 1, 0, where), picked(cotangent, 1, 1, where)
    token_rest[2], token_rest[3], token_first = tie((token_rest[2], token_rest[3], token_first))
    token_first, grad_rows = to_heads(token_first), to_heads(grad_rows)
    token_rest, token_first[0], grad_rows[0], joined = tie((token_rest, token_first[0], grad_rows[0], joined))

    half_chunks, full_chunks = ((576, 128), BF), ((16, 72, 128), BF)
    halves = [((2304, 128), F32), ((4, 576, 128), BF)]
    wide, half, short = ((3 * PER_HEAD, 128), BF), ((768, 128), BF), ((240, 128), BF)
    rest_shape, second_shape, third_shape = ((8, 240, 128), BF), ((8, 192, 128), BF), ((8, 48, 128), BF)
    whole_first, whole_rest = ((768, WIDTH), BF), ((240, WIDTH), BF)
    slot = ((SLOT, WIDTH), BF)

    x_rest, query_rest, rest = call(
        project_rest_kernel, [whole_rest, short, rest_shape], flops=2 * 240 * 768 * 256
    )(*token_rest, joined)
    rest, token_first[2] = tie((rest, token_first[2]))
    rest = deal(rest, "z")
    x_first, query_first, first = call(
        project_first_kernel, [whole_first, half, half], flops=2 * 768 * 768 * 256
    )(*token_first, joined)
    first_other = swap(first, "z", 1)
    third, x_first = tie((rest[:, 192:240], x_first))
    thirds = [swap(third, "x", j) for j in (1, 2, 3)]
    c_first, c_rest, grads = call(
        grad_rows_kernel, [whole_first, whole_rest, wide], flops=2 * 1008 * 768 * 128
    )(*grad_rows, w_out)

    attended, query_grad, first_back, first_send, second_back, *third_back = call(
        attention_kernel,
        [wide, wide, half, half, second_shape] + [third_shape] * 4,
        scratch=[((9, 512, 128), BF)],
        smem=2,
        flops=2 * 1008 * 512 * 128 * 7,
    )(offsets, where, query_first, query_rest, grads, first, first_other, rest, *thirds)

    third_got = [third_back[0]] + [swap(third_back[j], "x", j) for j in (1, 2, 3)]
    first_got = swap(first_send, "z", 1)
    early = call(early_kernel, [half_chunks] * 4, scratch=halves, smem=1, flops=4 * 1008 * 768 * 128)(
        where, attended, query_grad, c_first, c_rest, x_first, x_rest
    )
    mixed_slots = call(output_kernel, [slot] * 4, flops=2 * 1008 * 768 * 128)(attended, w_out)
    mixed_slots = to_heads(mixed_slots)
    early = [early[0]] + [swap(early[k], "x", k) for k in (1, 2, 3)]
    third_got, first_got, mixed_slots[0], early[0] = tie((third_got, first_got, mixed_slots[0], early[0]))
    (rest_back,) = call(third_sum_kernel, [rest_shape])(second_back, *third_got)
    rest_got = deal(rest_back, "z")
    rest_got, early = tie((rest_got, early))

    *late, changes = call(
        change_kernel,
        [half_chunks] * 4 + [((3 * PER_HEAD, 256), BF)],
        scratch=halves,
        smem=1,
        flops=2 * 1008 * 768 * 128,
    )(where, first_back, first_got, rest_got, query_grad, x_first, x_rest)
    late = [late[0]] + [swap(late[k], "x", k) for k in (1, 2, 3)]
    change_slots = call(input_kernel, [slot] * 4, flops=2 * 1008 * 768 * 256)(changes, joined)
    spread = call(spread_kernel, [((ROWS, WIDTH), BF)], smem=2, flops=2 * 1024 * 512 * 768)
    late, mixed_slots, change_slots = tie((late, mixed_slots, change_slots))
    (parts,) = call(x_sum_kernel, [full_chunks], scratch=[((2, 576, 128), F32), ((72, 128), F32)])(*early, *late)
    (part,) = call(yz_sum_kernel, [full_chunks])(deal(parts, YZ_AXES))
    (mixed,) = spread(offsets, where, *mixed_slots)
    part, mixed, change_slots = tie((part, mixed, change_slots))
    block, change_slots = deal(part, YZ_AXES), to_heads(change_slots)
    blocks = [block] + [swap(block, "x", k) for k in (1, 2, 3)]
    (grad_tokens,) = spread(offsets, where, *change_slots)
    grad_query, grad_out, grad_key, grad_value = call(
        place_kernel,
        [((192, WIDTH), F32)] * 4,
        scratch=[((4, 16, 72, 128), BF), ((72, 128), F32), ((2, 2304, 128), F32)],
        smem=1,
    )(where, *blocks)
    return mixed, grad_tokens, grad_query, grad_key, grad_value, grad_out


def solution(mesh):
    fine = jax.sharding.Mesh(mesh.devices.reshape(2, 4, 8, 2, 2), ("yh", "x", "z", "yl", "core"))
    rows = P(("yh", "x", "z", "yl", "core"), None)
    cut = P(HEAD_AXES, None)
    return jax.shard_map(
        per_device,
        mesh=fine,
        in_specs=(rows, rows, cut, cut, cut, cut, P()),
        out_specs=(rows, rows, cut, cut, cut, cut),
        check_vma=False,
    )
```
